32 devices in a mesh: gx: 4 (over z), gy: 8 (over y, x, core).
Axes of the slice: x: 2, y: 2, z: 4, core: 2. Of those that a mesh axis runs over, the one named last changes fastest.
Arguments:
- child_coef: bfloat16 [64, 16, 128, 128], P(('gx', 'gy')), may hold values from -6 to 6
- transfer: bfloat16 [64, 64, 2, 128, 128], P(('gx', 'gy')), may hold values from -0.125 to 0.125
- child_dir: int32 [64, 64], P(('gx', 'gy')), may hold values from 0 to 15, as said below
- couple_src: int32 [8, 64, 7], P('gx', 'gy'), may hold values from 0 to 7, as said below
- couple_kind: int32 [8, 64, 7], P('gx', 'gy'), may hold values from 0 to 7
- couple_count: int32 [8, 64], P('gx', 'gy'), may hold values from 1 to 7, as said below
- couple_table: bfloat16 [64, 8, 2, 128, 128], P('gy'), may hold values from -0.1875 to 0.1875
Outputs:
- child_local: bfloat16 [64, 16, 128, 128], P(('gx', 'gy'))
The draws below stay inside these ranges and needn't reach their ends.
Inputs may be any that keep to these rules, and one draw needn't show every extreme that they name: `child_dir`: in every row each child direction is named by exactly four parent directions. `couple_src`: the entries of one block row are distinct and never the row's own parent cluster. `couple_count`: some row holds 7.
All inputs are finite; a program needn't handle non-finite values.
Results may differ from the reference program's by a relative error of at most 0.015.
Values may be sent and summed in bfloat16 or wider, within the bound.
No kernel may reach another device: no remote copies, remote signals or barrier semaphores. Data moves between devices by JAX's collectives and lax.ppermute only.
A program may use at most 128 MiB of HBM per device.

```python
import jax
import jax.numpy as jnp
from jax import lax

R = 128
A = 64
CPD = 2
DP = 64
MAXC = 7
NOFF = 8
DC = 16
CLUSTERS = 64
PARENTS = 8


def draw_child_dir(key, part):
    subkeys = jax.random.split(key, CLUSTERS)

    def shuffle_one(subkey):
        return jax.random.permutation(subkey, DP)
    shuffled = jax.vmap(shuffle_one)(subkeys)
    return (shuffled % DC).astype(jnp.int32)


def draw_couple_src(key, part):
    subkeys = jax.random.split(key, PARENTS * DP)

    def pick_row(subkey):
        return jax.random.permutation(subkey, PARENTS - 1)[:MAXC]
    chosen = jax.vmap(pick_row)(subkeys).reshape((PARENTS, DP, MAXC)).astype(jnp.int32)
    own_row = jnp.arange(PARENTS, dtype=jnp.int32)[:, None, None]
    return jnp.where(chosen >= own_row, chosen + 1, chosen).astype(jnp.int32)


def draw_couple_count(key, part):
    counts = jax.random.randint(key, (PARENTS, DP), 1, MAXC + 1).astype(jnp.int32)
    return counts.at[0, 0].set(MAXC).astype(jnp.int32)


def touch_ends(entries, key, least, largest):
    index_at = [jax.random.randint(jax.random.fold_in(key, axis), (), 0, length) for axis, length in enumerate(entries.shape)]
    widest = entries.shape.index(max(entries.shape))
    beside = index_at[:widest] + [(index_at[widest] + 1) % entries.shape[widest]] + index_at[widest + 1:]
    return entries.at[tuple(index_at)].set(least).at[tuple(beside)].set(largest)


def block_levels(key, extent, shards, low, top_value):
    def one(dim, blocks):
        heights = jax.random.uniform(jax.random.fold_in(jax.random.fold_in(key, 6), dim), (blocks,), jnp.float32, low / len(shards), top_value / len(shards))
        return jnp.repeat(jnp.exp(heights), extent[dim] // blocks).reshape((-1,) + (1,) * (len(extent) - dim - 1))

    loudness = one(*shards[0])
    for cut in shards[1:]:
        loudness = loudness * one(*cut)
    return loudness


def scatter_about(own_key, dims, scale, bound, cuts=(), kind=jnp.bfloat16):
    drawn = jax.random.normal(own_key, dims, jnp.float32) * scale
    if len(cuts) > 0:
        drawn = block_levels(own_key, dims, cuts, -0.22, 0.18) * drawn
    return jnp.clip(drawn, min=-bound, max=bound).astype(kind)


def setup_inputs(seed: int = 0) -> dict:
    splits = jax.random.split(jax.random.key(seed), 8)
    child_coef = scatter_about(splits[0], (CLUSTERS, DC, R, 2 * A), 1.0, 6.0, ((0, 32),))
    transfer = scatter_about(splits[1], (CLUSTERS, DP, 2, R, R), (16 * R) ** -0.5, 0.125, ((0, 32),))
    child_dir = draw_child_dir(jax.random.fold_in(splits[7], 71), 0)
    couple_src = draw_couple_src(jax.random.fold_in(splits[7], 71), 0)
    couple_kind = touch_ends(jax.random.randint(splits[4], (PARENTS, DP, MAXC), 0, NOFF), jax.random.fold_in(splits[4], 1), 0, NOFF - 1).astype(jnp.int32)
    couple_count = draw_couple_count(jax.random.fold_in(splits[7], 71), 0)
    couple_table = scatter_about(splits[6], (DP, NOFF, 2, R, R), (R * (MAXC + 1)) ** -0.5, 0.1875, ((0, 8),))
    return dict(child_coef=child_coef, transfer=transfer, child_dir=child_dir, couple_src=couple_src, couple_kind=couple_kind, couple_count=couple_count, couple_table=couple_table)


def complex_apply(real_part, imag_part, vectors, pattern):
    halfway = vectors.shape[-1] // 2
    vectors = vectors.astype(jnp.float32)
    real_term = jnp.einsum(pattern, real_part.astype(jnp.float32), vectors, precision=lax.Precision.HIGHEST)
    imag_term = jnp.einsum(pattern, imag_part.astype(jnp.float32), vectors, precision=lax.Precision.HIGHEST)
    return jnp.concatenate([real_term[..., :halfway] - imag_term[..., halfway:], real_term[..., halfway:] + imag_term[..., :halfway]], axis=-1)


def reference(child_coef, transfer, child_dir, couple_src, couple_kind, couple_count, couple_table):
    coef_groups = child_coef.reshape((PARENTS, 8, DC, R, 2 * A))
    transfer_groups = transfer.reshape((PARENTS, 8, DP, 2, R, R))
    dir_groups = child_dir.reshape((PARENTS, 8, DP)).astype(jnp.int32)

    def ascend(inputs):
        coefs, matrices, directions = inputs
        picked = jnp.take_along_axis(coefs, directions[:, :, None, None], axis=1)
        up_term = complex_apply(matrices[:, :, 0], matrices[:, :, 1], picked, "kers,kesa->kera")
        grouped = up_term.reshape((8 // CPD, CPD, DP, R, 2 * A))
        group_sum = jnp.sum(grouped, axis=1).astype(jnp.bfloat16)
        return jnp.sum(group_sum.astype(jnp.float32), axis=0).astype(jnp.bfloat16)

    parent = lax.map(ascend, (coef_groups, transfer_groups, dir_groups))
    dir_index = jnp.arange(DP, dtype=jnp.int32)[:, None]
    slot_index = jnp.arange(MAXC, dtype=jnp.int32)[None, :]

    def couple(inputs):
        sources_row, kinds_row, counts_row = inputs
        sources = parent[sources_row.astype(jnp.int32), dir_index]
        matrices = couple_table[dir_index, kinds_row.astype(jnp.int32)]
        products = complex_apply(matrices[:, :, 0], matrices[:, :, 1], sources, "emrs,emsa->emra")
        active = slot_index < counts_row[:, None]
        return jnp.sum(jnp.where(active[:, :, None, None], products, 0.0), axis=1).astype(jnp.bfloat16)

    parent_local = lax.map(couple, (couple_src, couple_kind, couple_count))
    child_index = jnp.arange(DC, dtype=jnp.int32)

    def descend(inputs):
        matrices, directions, local_row = inputs
        products = complex_apply(matrices[:, :, 0], matrices[:, :, 1], local_row, "kesr,esa->kera")
        onehot = (directions[:, None, :] == child_index[None, :, None]).astype(jnp.float32)
        return jnp.einsum("kie,kera->kira", onehot, products, precision=lax.Precision.HIGHEST).astype(jnp.bfloat16)

    child_local = lax.map(descend, (transfer_groups, dir_groups, parent_local))
    return child_local.reshape((CLUSTERS, DC, R, 2 * A))
```

```python
import functools

import jax
import jax.numpy as jnp
from jax import lax
from jax.experimental import pallas as pl
from jax.experimental.pallas import tpu as pltpu
from jax.sharding import PartitionSpec as P

F32 = jnp.float32
BF16 = jnp.bfloat16


def turned(v):
    half = v.shape[-1] // 2
    return jnp.concatenate([-v[..., half:], v[..., :half]], axis=-1)


def turned_rows(v):
    half = v.shape[0] // 2
    return jnp.concatenate([-v[half:], v[:half]], axis=0)


def dot(a, b):
    return jnp.dot(a, b, preferred_element_type=F32)


def up_kernel(rel, fam, me_ref, dir_ref, coef_ref, mat_ref, *rest):
    out_ref = rest[-1]
    children, _, _, zs, per = mat_ref.shape[:5]
    owner = pl.program_id(0) * fam + lax.bitwise_xor(me_ref[0], rel)
    first_z = pl.program_id(1) * zs
    span = pl.num_programs(1) * zs * per
    for z in range(zs):
        for m in range(per):
            e = owner * span + (first_z + z) * per + m
            total = None
            for c in range(children):
                v = coef_ref[c, dir_ref[c, e]]
                both = jnp.concatenate([mat_ref[c, 0, 0, z, m, 0], mat_ref[c, 0, 0, z, m, 1]], axis=1)
                term = dot(both, jnp.concatenate([v, turned(v)], axis=0))
                total = term if total is None else total + term
            for more in rest[:-1]:
                total = total + more[z, 0, m].astype(F32)
            out_ref[z, 0, m] = total.astype(BF16)


def up(rel, fam, zblock, me, dirs, coef, mats, adds):
    children, planes, _, nz, per, _, rank, _ = mats.shape
    width = coef.shape[-1]
    piece = pl.BlockSpec((zblock, 1, per, rank, width), lambda q, z, me, d: (z, q, 0, 0, 0))
    steps = (planes, nz // zblock)
    return pl.pallas_call(
        functools.partial(up_kernel, rel, fam),
        out_shape=jax.ShapeDtypeStruct((nz, planes, per, rank, width), BF16),
        grid_spec=pltpu.PrefetchScalarGridSpec(
            num_scalar_prefetch=2,
            grid=steps,
            in_specs=[
                pl.BlockSpec(coef.shape, lambda q, z, me, d: (0, 0, 0, 0)),
                pl.BlockSpec(
                    (children, 1, 1, zblock, per, 2, rank, rank),
                    lambda q, z, me, d: (0, q, lax.bitwise_xor(me[0], rel), z, 0, 0, 0, 0),
                ),
            ]
            + [piece] * len(adds),
            out_specs=piece,
        ),
        cost_estimate=pl.CostEstimate(
            flops=4 * children * planes * nz * per * rank * rank * width,
            bytes_accessed=children * planes * nz * per * rank * rank * 4,
            transcendentals=0,
        ),
        compiler_params=pltpu.CompilerParams(vmem_limit_bytes=32 << 20),
    )(me, dirs, coef, mats, *adds)


def add_kernel(*refs):
    total = refs[0][...].astype(F32)
    for ref in refs[1:-1]:
        total = total + ref[...].astype(F32)
    refs[-1][...] = total.astype(BF16)


def add(*arrays):
    shape = arrays[0].shape
    spec = pl.BlockSpec((1,) + shape[1:], lambda i: (i,) + (0,) * (len(shape) - 1))
    return pl.pallas_call(
        add_kernel,
        out_shape=jax.ShapeDtypeStruct(shape, BF16),
        grid=(shape[0],),
        in_specs=[spec] * len(arrays),
        out_specs=spec,
    )(*arrays)


def couple_kernel(at_ref, src_ref, kind_ref, count_ref, par_ref, table_ref, out_ref, wide):
    sources = par_ref.shape[0]
    rows = out_ref.shape[0]
    rank = par_ref.shape[2]
    most = src_ref.shape[0] // count_ref.shape[0]
    dirs_held = count_ref.shape[0] // rows
    slot = at_ref[0] + pl.program_id(0)

    def widen(t, carry):
        v = par_ref[t, 0]
        wide[t, :rank] = v
        wide[t, rank:] = turned(v)
        return carry

    lax.fori_loop(0, sources, widen, 0, unroll=min(sources, 8))
    wide[sources] = jnp.zeros_like(wide[sources])

    def one_row(t, carry):
        row = t * dirs_held + slot
        count = count_ref[row]
        total = None
        for k in range(most):
            kind = kind_ref[row * most + k]
            source = jnp.where(k < count, src_ref[row * most + k], sources)
            both = jnp.concatenate([table_ref[0, kind, 0], table_ref[0, kind, 1]], axis=1)
            term = dot(both, wide[source])
            total = term if total is None else total + term
        out_ref[t, 0] = total.T.astype(BF16)
        return carry

    lax.fori_loop(0, rows, one_row, 0, unroll=min(rows, 4))


def couple(at, src, kind, count, parents, table):
    sources, per, rank, width = parents.shape
    rows = src.shape[0]
    kinds = table.shape[1]
    return pl.pallas_call(
        couple_kernel,
        out_shape=jax.ShapeDtypeStruct((rows, per, width, rank), BF16),
        grid_spec=pltpu.PrefetchScalarGridSpec(
            num_scalar_prefetch=4,
            grid=(per,),
            in_specs=[
                pl.BlockSpec((sources, 1, rank, width), lambda m, at, *_: (0, m, 0, 0)),
                pl.BlockSpec((1, kinds, 2, rank, rank), lambda m, at, *_: (at[0] + m, 0, 0, 0, 0)),
            ],
            out_specs=pl.BlockSpec((rows, 1, width, rank), lambda m, at, *_: (0, m, 0, 0)),
            scratch_shapes=[pltpu.VMEM((sources + 1, 2 * rank, width), BF16)],
        ),
        cost_estimate=pl.CostEstimate(
            flops=4 * rows * per * src.shape[2] * rank * rank * width,
            bytes_accessed=per * kinds * 4 * rank * rank,
            transcendentals=0,
        ),
        compiler_params=pltpu.CompilerParams(vmem_limit_bytes=32 << 20),
    )(at, src.reshape(-1), kind.reshape(-1), count.reshape(-1), parents, table)


def down_kernel(me_ref, dir_ref, mat_ref, *rest):
    pieces, out_ref, sums = rest[:-2], rest[-2], rest[-1]
    children, _, fam, zs, per, _, rank, _ = mat_ref.shape
    first = jnp.logical_and(pl.program_id(0) == 0, pl.program_id(1) == 0)
    last = jnp.logical_and(
        pl.program_id(0) == pl.num_programs(0) - 1, pl.program_id(1) == pl.num_programs(1) - 1
    )
    first_z = pl.program_id(1) * zs
    span = pl.num_programs(1) * zs * per

    @pl.when(first)
    def _():
        sums[...] = jnp.zeros_like(sums)

    for rel, piece in enumerate(pieces):
        side = lax.bitwise_xor(me_ref[0], rel)
        owner = pl.program_id(0) * fam + side
        for z in range(zs):
            for m in range(per):
                e = owner * span + (first_z + z) * per + m
                v = piece[z, 0, m]
                x = jnp.concatenate([v, turned_rows(v)], axis=1)
                for c in range(children):
                    i = dir_ref[c, e]
                    sums[c, i] += dot(x, mat_ref[c, 0, side, z, m].reshape(2 * rank, rank))

    @pl.when(last)
    def _():
        for c in range(children):
            for i in range(out_ref.shape[1]):
                out_ref[c, i] = sums[c, i].T.astype(BF16)


def down(zblock, me, dirs, mats, pieces, groups):
    children, planes, fam, nz, per, _, rank, _ = mats.shape
    width = pieces[0].shape[-2]
    piece = pl.BlockSpec((zblock, 1, per, width, rank), lambda q, z, me, d: (z, q, 0, 0, 0))
    return pl.pallas_call(
        down_kernel,
        out_shape=jax.ShapeDtypeStruct((children, groups, rank, width), BF16),
        grid_spec=pltpu.PrefetchScalarGridSpec(
            num_scalar_prefetch=2,
            grid=(planes, nz // zblock),
            in_specs=[
                pl.BlockSpec(
                    (children, 1, fam, zblock, per, 2, rank, rank),
                    lambda q, z, me, d: (0, q, 0, z, 0, 0, 0, 0),
                )
            ]
            + [piece] * len(pieces),
            out_specs=pl.BlockSpec((children, groups, rank, width), lambda q, z, me, d: (0, 0, 0, 0)),
            scratch_shapes=[pltpu.VMEM((children, groups, width, rank), F32)],
        ),
        compiler_params=pltpu.CompilerParams(vmem_limit_bytes=32 << 20),
    )(me, dirs, mats, *pieces)


def body(nx, ny, child_coef, transfer, child_dir, couple_src, couple_kind, couple_count, couple_table):
    children, dirs, _, rank, _ = transfer.shape
    planes = couple_src.shape[0]
    fam = ny // planes
    held = dirs // ny
    split = held % nx == 0
    nz = nx if split else 1
    per = held // nz
    at_y, at_x = lax.axis_index("gy"), lax.axis_index("gx")
    side = lax.rem(at_y, fam).astype(jnp.int32).reshape(1)
    mats = transfer.reshape(children, planes, fam, nz, per, 2, rank, rank)
    zblock = min(nz, 2)

    def swap(x, rel):
        return lax.ppermute(x, "gy", [(i, i ^ rel) for i in range(ny)])

    def exchange(x):
        shape = x.shape
        if split:
            groups = [[z * ny + q * fam + j for z in range(nx) for q in range(planes)] for j in range(fam)]
            axes = ("gx", "gy")
        else:
            groups = [[q * fam + j for q in range(planes)] for j in range(fam)]
            axes = "gy"
        x = x.reshape((-1,) + shape[2:])
        x = lax.all_to_all(x, axes, split_axis=0, concat_axis=0, tiled=True, axis_index_groups=groups)
        return x.reshape(shape)

    if split:
        packed = jnp.concatenate([couple_src, couple_kind, couple_count[..., None]], axis=-1)
        packed = lax.all_gather(packed, "gx", axis=0, tiled=True)
        most = couple_src.shape[-1]
        src, kind, count = packed[..., :most], packed[..., most : 2 * most], packed[..., 2 * most]
        at = (at_x * per).astype(jnp.int32).reshape(1)
    else:
        src, kind, count = couple_src, couple_kind, couple_count
        at = jnp.zeros((1,), jnp.int32)

    one = functools.partial(up, fam=fam, zblock=zblock, me=side, dirs=child_dir, coef=child_coef, mats=mats)
    pending = {}
    kept = {}
    rels = list(range(fam))
    bit = 1
    sums = {}
    order = sorted(rels, key=lambda r: -r)
    got = {rel: [] for rel in rels}
    for rel in sorted(rels, key=lambda r: [-(r & (1 << b)) for b in range(fam.bit_length() - 1)] + [-r]):
        low = rel & -rel
        adds = got[rel]
        if rel:
            mine = one(rel, adds=adds)
            got[rel ^ low].append(swap(mine, low))
        else:
            base = one(rel, adds=[])
            whole = add(base, *adds)

    parents = exchange(whole)
    parents = parents.reshape((nz * planes, per) + parents.shape[3:])
    if not split:
        parents = lax.all_gather(parents, "gx", axis=0, tiled=True)
    local = couple(at, src, kind, count, parents, couple_table)
    local = local.reshape((nz, planes) + local.shape[1:])
    pieces = {0: exchange(local)}
    for rel in range(1, fam):
        high = 1 << (rel.bit_length() - 1)
        low = rel & -rel
        pieces[rel] = None
    step = fam // 2
    while step:
        for rel in sorted(r for r in pieces if pieces[r] is not None):
            if pieces.get(rel ^ step, 0) is None:
                pieces[rel ^ step] = swap(pieces[rel], step)
        step //= 2
    return down(zblock // 2 or 1, side, child_dir, mats, [pieces[r] for r in range(fam)], child_coef.shape[1])


def solution(mesh):
    return jax.shard_map(
        functools.partial(body, mesh.shape["gx"], mesh.shape["gy"]),
        mesh=mesh,
        in_specs=(
            P(("gx", "gy"), None, None, None),
            P(("gx", "gy"), None, None, None, None),
            P(("gx", "gy"), None),
            P("gx", "gy", None),
            P("gx", "gy", None),
            P("gx", "gy"),
            P("gy", None, None, None, None),
        ),
        out_specs=P(("gx", "gy"), None, None, None),
        check_vma=False,
    )
```

```python
import functools

import jax
import jax.numpy as jnp
from jax import lax
from jax.experimental import pallas as pl
from jax.experimental.pallas import tpu as pltpu
from jax.sharding import PartitionSpec as P

F32 = jnp.float32
BF16 = jnp.bfloat16
SMEM = pl.BlockSpec(memory_space=pltpu.SMEM)
VMEM = pl.BlockSpec(memory_space=pltpu.VMEM)
ANY = pl.BlockSpec(memory_space=pl.ANY)
COST = pl.CostEstimate(flops=10000000000, bytes_accessed=1000000, transcendentals=0)
PARAMS = pltpu.CompilerParams(vmem_limit_bytes=16 << 20)


def turned(v):
    half = v.shape[-1] // 2
    return jnp.concatenate([-v[..., half:], v[..., :half]], axis=-1)


def turned_rows(v):
    half = v.shape[0] // 2
    return jnp.concatenate([-v[half:], v[:half]], axis=0)


def dot(a, b):
    return jnp.dot(a, b, preferred_element_type=F32)


def xor(a, b):
    return lax.bitwise_xor(a, jnp.int32(b))


def place(at_ref, planes, rel, base, core):
    turn = lax.bitwise_and(xor(at_ref[1], rel), jnp.int32(1))
    q = lax.bitwise_xor(xor(at_ref[0], base % planes), turn)
    return q, xor(at_ref[1], rel ^ core), xor(at_ref[2], base // planes)


def up_kernel(groups, fetches, at_ref, dir_ref, coef_hbm, mat_hbm, *rest):
    table_hbm, rest = (rest[0], rest[1:]) if fetches else (None, rest)
    outs, (coef_ref, mat_ref, coef_sem, mat_sem) = rest[:-4], rest[-4:]
    children, planes, fam, nz, per = mat_hbm.shape[:5]

    def start(group, first):
        copies = []
        for out, rel, bases in group:
            for n, core in [(n, core) for n in range(len(bases)) for core in range(2)]:
                q, j, z = place(at_ref, planes, rel, bases[n], core)
                slot = first + len(copies)
                copy = pltpu.make_async_copy(mat_hbm.at[:, q, j, z], mat_ref.at[slot], mat_sem.at[slot])
                copy.start()
                copies.append((copy, outs[out], (n, core), ((q * fam + j) * nz + z) * per, slot))
        return copies

    coef_copy = pltpu.make_async_copy(coef_hbm, coef_ref, coef_sem)
    coef_copy.start()
    flying, first = [], 0
    for group in groups[:2]:
        flying.append(start(group, first))
        first += len(flying[-1])
    coef_copy.wait()
    for n in range(len(groups)):
        for copy, *_ in flying[n]:
            copy.wait()
        if n + 2 < len(groups):
            flying.append(start(groups[n + 2], first))
            first += len(flying[-1])
        elif n + 2 == len(groups) and fetches:
            table_copy = pltpu.make_async_copy(table_hbm.at[pl.ds(at_ref[2] * per, per)], outs[-1], coef_sem)
            table_copy.start()
        for _, out, spot, e, slot in flying[n]:
            for m in range(per):
                left, right = [], []
                for c in range(children):
                    v = coef_ref[c, dir_ref[c, e + m]]
                    left += [mat_ref[slot, c, m, 0], mat_ref[slot, c, m, 1]]
                    right += [v, turned(v)]
                out[spot + (m,)] = dot(jnp.concatenate(left, axis=1), jnp.concatenate(right, axis=0)).astype(BF16)
    if fetches:
        table_copy.wait()


def up(at, dirs, coef, mats, halves, groups, table=None):
    children, planes, fam, nz, per, _, rank, _ = mats.shape
    width = coef.shape[-1]
    names = [name for group in groups for name in group]
    jobs = [[(names.index((h, rel)), rel, halves[h]) for h, rel in group] for group in groups]
    slots = 2 * sum(len(halves[h]) for h, _ in names)
    extra = [] if table is None else [table]
    found = pl.pallas_call(
        functools.partial(up_kernel, jobs, len(extra)),
        out_shape=[jax.ShapeDtypeStruct((len(halves[h]), 2, per, rank, width), BF16) for h, _ in names]
        + [jax.ShapeDtypeStruct((per,) + t.shape[1:], BF16) for t in extra],
        in_specs=[SMEM, SMEM] + [ANY] * (2 + len(extra)),
        out_specs=[VMEM] * (len(names) + len(extra)),
        scratch_shapes=[
            pltpu.VMEM(coef.shape, BF16),
            pltpu.VMEM((slots, children, per, 2, rank, rank), BF16),
            pltpu.SemaphoreType.DMA,
            pltpu.SemaphoreType.DMA((slots,)),
        ],
        compiler_params=PARAMS,
        cost_estimate=COST,
    )(at, dirs, *[pltpu.with_memory_space_constraint(x, pltpu.HBM) for x in [coef, mats] + extra])
    return dict(zip(names, found)), found[len(names) :]


def add_kernel(*refs):
    total = refs[0][...].astype(F32)
    for ref in refs[1:-1]:
        total = total + ref[...].astype(F32)
    refs[-1][...] = total.astype(BF16)


def add(arrays):
    return pl.pallas_call(
        add_kernel,
        out_shape=jax.ShapeDtypeStruct(arrays[0].shape, BF16),
        in_specs=[VMEM] * len(arrays),
        out_specs=VMEM,
        compiler_params=PARAMS,
        cost_estimate=COST,
    )(*arrays)


def part_kernel(count, *refs):
    lists, outs = refs[:2], refs[2 + count :]
    total = refs[2][...].astype(F32)
    for ref in refs[3 : 2 + count]:
        total = total + ref[...].astype(F32)
    total = total.astype(BF16)
    rows = total.shape[2] * total.shape[3]
    for n, out in enumerate(outs):
        for core in range(2):
            out[core, :rows] = total[n, core].reshape(rows, total.shape[4])
            out[core, rows:] = lists[core][...]


def part(arrays, lists):
    count, _, per, rank, width = arrays[0].shape
    return pl.pallas_call(
        functools.partial(part_kernel, len(arrays)),
        out_shape=[jax.ShapeDtypeStruct((2, per * rank + lists[0].shape[0], width), BF16)] * count,
        in_specs=[VMEM] * (2 + len(arrays)),
        out_specs=[VMEM] * count,
        compiler_params=PARAMS,
        cost_estimate=COST,
    )(*lists, *arrays)


def stack_kernel(core, *refs):
    for n, ref in enumerate(refs[:-1]):
        refs[-1][n] = ref[...] if core is None else ref[core]


def stack(arrays, core=None):
    shape = arrays[0].shape if core is None else arrays[0].shape[1:]
    return pl.pallas_call(
        functools.partial(stack_kernel, core),
        out_shape=jax.ShapeDtypeStruct((len(arrays),) + shape, arrays[0].dtype),
        in_specs=[VMEM] * len(arrays),
        out_specs=VMEM,
        compiler_params=PARAMS,
        cost_estimate=COST,
    )(*arrays)


def join_kernel(own_ref, other_ref, *outs):
    for n, out in enumerate(outs):
        out[0] = own_ref[n]
        out[1] = other_ref[n]


def join(own, other):
    return pl.pallas_call(
        join_kernel,
        out_shape=[jax.ShapeDtypeStruct((2,) + own.shape[1:], own.dtype)] * own.shape[0],
        in_specs=[VMEM] * 2,
        out_specs=[VMEM] * own.shape[0],
        compiler_params=PARAMS,
        cost_estimate=COST,
    )(own, other)


def couple_kernel(sizes, jobs, at_ref, *refs):
    planes, nz, most, held, halves, given = sizes
    me = lax.bitwise_and(at_ref[1], jnp.int32(1))
    first = given > 0
    if first:
        table_ref, own_ref = refs[:2]
        sources, refs = refs[2 : 2 + given], refs[2 + given :]
        rows, (wide, numbers, lists, sem) = refs[:-4], refs[-4:]
    else:
        lists, table_ref, wide = refs[:3]
        rows = refs[3:]
    per, _, _, rank, _ = table_ref.shape
    count = wide.shape[0] - 1
    if first:
        held_by, gathered = {}, []
        pos = 0
        for bases in halves:
            other = sources[pos + len(bases)]
            for n, base in enumerate(bases):
                held_by[base] = (sources[pos + n].at[0], other.at[n])
            pos += len(bases) + 1
        gathered = sources[pos:]
        numbers[0] = own_ref[...].astype(F32).astype(jnp.int32)
        for z in range(1, nz):
            mine, theirs = (ref[per * rank :].astype(F32) for ref in held_by[z * planes])
            numbers[z] = jnp.where(me == 0, mine, theirs).astype(jnp.int32)
        copy = pltpu.make_async_copy(numbers, lists, sem)
        copy.start()
        parts = []
        if gathered:
            parts = [(t, gathered[0].at[t]) for t in range(gathered[0].shape[0])]
        else:
            for base, pair in held_by.items():
                for s, source in enumerate(pair):
                    q = lax.bitwise_xor(xor(at_ref[0], base % planes), xor(me, s))
                    parts.append((xor(at_ref[2], base // planes) * planes + q, source))
        for t, source in parts:
            for m in range(per):
                v = source[m * rank : (m + 1) * rank]
                wide[t, m, :rank] = v
                wide[t, m, rank:] = turned(v)
        wide[count] = jnp.zeros_like(wide[count])
        copy.wait()
    for row, (bases, s) in zip(rows, jobs):
        for n, base in enumerate(bases):
            q, z = lax.bitwise_xor(xor(at_ref[0], base % planes), xor(me, s)), at_ref[2]
            for m in range(per):
                entry = (base // planes, q * held + z * per + m)
                active = lists[entry + (2 * most,)]
                total = None
                for k in range(most):
                    kind = lists[entry + (most + k,)]
                    source = jnp.where(k < active, lists[entry + (k,)], count)
                    both = jnp.concatenate([table_ref[m, kind, 0], table_ref[m, kind, 1]], axis=1)
                    term = dot(both, wide[source, m])
                    total = term if total is None else total + term
                row[n, m] = total.T.astype(BF16)


def couple(at, table, jobs, sizes, own=None, sources=(), total=0, lists=None, wide=None):
    per, _, _, rank, _ = table.shape
    width = (sources[0] if sources else wide).shape[-1]
    rows = [jax.ShapeDtypeStruct((len(bases), per, width, rank), BF16) for bases, _ in jobs]
    grown, scratch = [], []
    if sources:
        listed = (sizes[1],) + own.shape
        grown = [
            jax.ShapeDtypeStruct((total + 1, per, 2 * rank, width), BF16),
            jax.ShapeDtypeStruct(listed, jnp.int32),
        ]
        scratch = [pltpu.SMEM(listed, jnp.int32), pltpu.SemaphoreType.DMA]
    return pl.pallas_call(
        functools.partial(couple_kernel, sizes + (len(sources),), jobs),
        out_shape=rows + grown,
        in_specs=[SMEM] + ([VMEM] * (2 + len(sources)) if sources else [SMEM, VMEM, VMEM]),
        out_specs=[VMEM] * (len(rows) + len(grown)),
        scratch_shapes=scratch,
        compiler_params=PARAMS,
        cost_estimate=COST,
    )(at, *((table, own, *sources) if sources else (lists, table, wide)))


def down_kernel(jobs, last, at_ref, dir_ref, mat_ref, *rest):
    pieces = rest[: len(jobs)]
    if last:
        before, out_ref, sums = rest[len(jobs) :]
    else:
        (sums,) = rest[len(jobs) :]
    children, planes, fam, nz, per, _, rank, _ = mat_ref.shape
    sums[...] = jnp.zeros_like(sums)
    for piece, (rel, bases) in zip(pieces, jobs):
        for n, core in [(n, core) for n in range(len(bases)) for core in range(2)]:
            q, j, z = place(at_ref, planes, rel, bases[n], core)
            for m in range(per):
                e = ((q * fam + j) * nz + z) * per + m
                v = piece[n, core, m]
                x = jnp.concatenate([v, turned_rows(v)], axis=1)
                both = [mat_ref[c, q, j, z, m].reshape(2 * rank, rank) for c in range(children)]
                y = dot(x, jnp.concatenate(both, axis=1))
                for c in range(children):
                    sums[c, dir_ref[c, e]] += y[:, c * rank : (c + 1) * rank]
    if last:
        for c in range(children):
            for i in range(out_ref.shape[1]):
                out_ref[c, i] = (sums[c, i] + before[c, i]).T.astype(BF16)


def down(at, dirs, mats, jobs, pieces, groups, before=None):
    children, rank = mats.shape[0], mats.shape[-1]
    width = pieces[0].shape[-2]
    last = before is not None
    sums = (children, groups, width, rank)
    return pl.pallas_call(
        functools.partial(down_kernel, jobs, last),
        out_shape=jax.ShapeDtypeStruct((children, groups, rank, width), BF16) if last else jax.ShapeDtypeStruct(sums, F32),
        in_specs=[SMEM, SMEM] + [VMEM] * (1 + len(pieces) + (1 if last else 0)),
        out_specs=VMEM,
        scratch_shapes=[pltpu.VMEM(sums, F32)] if last else [],
        compiler_params=PARAMS,
        cost_estimate=COST,
    )(at, dirs, mats, *pieces, *([before] if last else []))


def body(nx, ny, child_coef, transfer, child_dir, couple_src, couple_kind, couple_count, couple_table):
    children, dirs, _, rank, _ = transfer.shape
    planes, held, most = couple_src.shape
    fam = ny // planes
    split = held % nx == 0
    nz = nx if split else 1
    per = held // nz
    partners = nz * planes
    at_y, at_x = lax.axis_index("gy"), lax.axis_index("gx")
    at = jnp.stack([at_y // fam, at_y % fam, at_x if split else jnp.zeros_like(at_x)]).astype(jnp.int32)
    mats = transfer.reshape(children, planes, fam, nz, per, 2, rank, rank)
    bases = tuple(range(partners - 2, -1, -2))
    far, near = bases[: len(bases) // 2], bases[len(bases) // 2 :]
    halves = (far, near)

    def family(x, rel):
        return lax.ppermute(x, "gy", [(i, i ^ rel) for i in range(ny)])

    def partner(x, base):
        moves = [(r // planes) * ny + (r % planes) * fam for r in (base, base ^ 1)]
        axes, size = (("gx", "gy"), nx * ny) if split else ("gy", ny)
        return lax.ppermute(x, axes, [(i, i ^ moves[i & 1]) for i in range(size)])

    lists = jnp.concatenate([couple_src, couple_kind, couple_count[..., None]], axis=-1).reshape(planes * held, -1)
    lists = jnp.pad(lists, ((0, -planes * held % 16), (0, rank - lists.shape[1]))).astype(BF16)
    odd = [rel for rel in range(fam) if rel & 1]
    lead = [(0, odd[-1])]
    soon = [[(0, odd[-1] ^ 1), (1, odd[-1])], [(0, rel) for rel in odd[:-1]]]
    early = lead + soon[0] + soon[1]
    late = [(h, rel) for h in (1, 0) for rel in sorted(range(fam), reverse=True) if (h, rel) not in early]
    got = {}
    sums, _ = up(at, child_dir, child_coef, mats, halves, [lead] + [group for group in soon if group])
    got.update({key: [value] for key, value in sums.items()})

    def reduce_step(h, rel):
        terms = got.pop((h, rel))
        low = rel & -rel
        got.setdefault((h, rel ^ low), []).append(family(add(terms) if len(terms) > 1 else terms[0], low))

    for key in early:
        if key[1] & 1:
            reduce_step(*key)
    key = (0, odd[-1] ^ 1)
    if key[1]:
        got[key] = [add(got[key])]
        got[key][0], at_late, lists = lax.optimization_barrier((got[key][0], at, lists))
        both_lists = (lists, family(lists, 1))
        reduce_step(*key)
    else:
        at_late = at
    late = [late[:1], late[1:3], late[3:5], late[5:]]
    sums, (table,) = up(at_late, child_dir, child_coef, mats, halves, [group for group in late if group], couple_table)
    for key, value in sums.items():
        got.setdefault(key, []).append(value)
    for rel in sorted((r for r in range(1, fam)), key=lambda r: (-(r & 1), -r)):
        if (0, rel) in got:
            reduce_step(0, rel)
        if rel & 1 and (1, rel) in got:
            reduce_step(1, rel)
    far_sent = part(got[(0, 0)], both_lists)
    for rel in range(fam - 2, 0, -2):
        got[(1, rel)], far_sent = lax.optimization_barrier((got[(1, rel)], far_sent))
        reduce_step(1, rel)
    sources = []
    for h, sent in ((0, far_sent), (1, part(got[(1, 0)], both_lists))):
        arrived = [partner(x, base) for x, base in zip(sent, halves[h])]
        sources += arrived + [family(stack(arrived, core=1), 1)]
    if not split:
        own = jnp.zeros((partners,) + sources[0].shape[1:], BF16)
        pos = 0
        for h in range(2):
            for n, base in enumerate(halves[h]):
                for s, value in enumerate((sources[pos + n][0], sources[pos + len(halves[h])][n])):
                    spot = lax.bitwise_xor(at[0], jnp.int32(base ^ s)) ^ (at[1] & 1)
                    own = lax.dynamic_update_index_in_dim(own, value, spot, 0)
            pos += len(halves[h]) + 1
        sources.append(lax.all_gather(own, "gx", axis=0, tiled=True))
    sizes = (planes, nz, most, held, halves)
    theirs, wide, numbers = couple(at, table, ((far, 1),), sizes, lists, sources, nx * planes)
    rows = {}
    theirs = family(theirs, 1)
    (mine,) = couple(at, table, ((far, 0),), sizes, lists=numbers, wide=wide)
    rows[0] = (mine, theirs)
    theirs, mine = couple(at, table, ((near, 1), (near, 0)), sizes, lists=numbers, wide=wide)
    rows[1] = (mine, family(theirs, 1))
    local = {}
    for h in range(2):
        for base, x in zip(halves[h], join(*rows[h])):
            local[base] = partner(x, base)
    pieces = {}
    for h in (1, 0):
        pieces[(h, 0)] = stack([local[r] for r in halves[h]])
    groups = child_coef.shape[1]

    def jobs(keys):
        return tuple((rel, halves[h]) for h, rel in keys)

    def spread(h, bit):
        for rel in sorted(r for g, r in pieces if g == h):
            pieces[(h, rel ^ bit)] = family(pieces[(h, rel)], bit)

    bits = [1 << n for n in range(fam.bit_length() - 1)]
    high = bits[-1]
    spread(1, high)
    for bit in bits[-2::-1]:
        pieces[(1, bit)] = family(pieces[(1, 0)], bit)
        pieces[(0, 0)], pieces[(1, bit)] = lax.optimization_barrier((pieces[(0, 0)], pieces[(1, bit)]))
    spread(0, high)
    for bit in bits[-2::-1]:
        for rel in sorted(r for g, r in pieces if g == 1):
            if (1, rel ^ bit) not in pieces:
                pieces[(1, rel ^ bit)] = family(pieces[(1, rel)], bit)
    straight = family(pieces[(0, 0)], 1) if fam > 2 else None
    first_keys = [key for key in pieces if key != (0, high)]
    values = [pieces[key] for key in first_keys]
    first_jobs = jobs(first_keys)
    if straight is not None:
        values.append(straight)
        first_jobs += ((1, far),)
    first = down(at, child_dir, mats, first_jobs, values, groups)
    pieces[(0, high)], first = lax.optimization_barrier((pieces[(0, high)], first))
    for bit in bits[-2::-1]:
        for rel in sorted(r for g, r in pieces if g == 0):
            if (0, rel ^ bit) not in pieces and not (bit == 1 and rel == 0):
                pieces[(0, rel ^ bit)] = family(pieces[(0, rel)], bit)
    last_keys = [key for key in pieces if key not in first_keys]
    return down(at, child_dir, mats, jobs(last_keys), [pieces[key] for key in last_keys], groups, before=first)


def solution(mesh):
    return jax.shard_map(
        functools.partial(body, mesh.shape["gx"], mesh.shape["gy"]),
        mesh=mesh,
        in_specs=(
            P(("gx", "gy"), None, None, None),
            P(("gx", "gy"), None, None, None, None),
            P(("gx", "gy"), None),
            P("gx", "gy", None),
            P("gx", "gy", None),
            P("gx", "gy"),
            P("gy", None, None, None, None),
        ),
        out_specs=P(("gx", "gy"), None, None, None),
        check_vma=False,
    )
```

```python
import functools

import jax
import jax.numpy as jnp
from jax import lax
from jax.experimental import pallas as pl
from jax.experimental.pallas import tpu as pltpu
from jax.sharding import PartitionSpec as P

F32 = jnp.float32
BF16 = jnp.bfloat16
SMEM = pl.BlockSpec(memory_space=pltpu.SMEM)
VMEM = pl.BlockSpec(memory_space=pltpu.VMEM)
ANY = pl.BlockSpec(memory_space=pl.ANY)
COST = pl.CostEstimate(flops=10000000000, bytes_accessed=1000000, transcendentals=0)
PARAMS = pltpu.CompilerParams(vmem_limit_bytes=16 << 20)


def turned(v):
    half = v.shape[-1] // 2
    return jnp.concatenate([-v[..., half:], v[..., :half]], axis=-1)


def turned_rows(v):
    half = v.shape[0] // 2
    return jnp.concatenate([-v[half:], v[:half]], axis=0)


def dot(a, b):
    return jnp.dot(a, b, preferred_element_type=F32)


def xor(a, b):
    return lax.bitwise_xor(a, jnp.int32(b))


def place(at_ref, planes, rel, base, core):
    turn = lax.bitwise_and(xor(at_ref[1], rel), jnp.int32(1))
    q = lax.bitwise_xor(xor(at_ref[0], base % planes), turn)
    return q, xor(at_ref[1], rel ^ core), xor(at_ref[2], base // planes)


def up_kernel(groups, at_ref, dir_ref, coef_hbm, mat_hbm, table_hbm, *rest):
    outs, (coef_ref, mat_ref, coef_sem, mat_sem) = rest[:-4], rest[-4:]
    children, planes, fam, nz, per = mat_hbm.shape[:5]

    coef_copy = pltpu.make_async_copy(coef_hbm, coef_ref, coef_sem)
    coef_copy.start()
    slots, flying = {}, []

    def start(group):
        copies = []
        for _, _, rel, bases in group:
            for base, core in [(base, core) for base in bases for core in range(2)]:
                key = (rel, core, base % planes)
                if key not in slots:
                    slots[key] = slot = len(slots)
                    q, j, _ = place(at_ref, planes, rel, base, core)
                    copies.append(pltpu.make_async_copy(mat_hbm.at[:, q, j], mat_ref.at[slot], mat_sem.at[slot]))
                    copies[-1].start()
        flying.append(copies)

    for group in groups[:2]:
        start(group)
    coef_copy.wait()
    for number, group in enumerate(groups):
        for copy in flying[number]:
            copy.wait()
        if number + 2 < len(groups):
            start(groups[number + 2])
        elif number + 2 == len(groups):
            table_copy = pltpu.make_async_copy(table_hbm.at[pl.ds(at_ref[2] * per, per)], outs[-1], coef_sem)
            table_copy.start()
        for out, offset, rel, bases in group:
            for n, core in [(n, core) for n in range(len(bases)) for core in range(2)]:
                q, j, z = place(at_ref, planes, rel, bases[n], core)
                slot = slots[rel, core, bases[n] % planes]
                for m in range(per):
                    left, right = [], []
                    for c in range(children):
                        v = coef_ref[c, dir_ref[c, ((q * fam + j) * nz + z) * per + m]]
                        left += [mat_ref[slot, c, z, m, 0], mat_ref[slot, c, z, m, 1]]
                        right += [v, turned(v)]
                    total = dot(jnp.concatenate(left, axis=1), jnp.concatenate(right, axis=0))
                    outs[out][offset + n, core, m] = total.astype(BF16)
    table_copy.wait()


def up(at, dirs, coef, mats, table, chunks, outs, groups):
    children, planes, fam, nz, per, _, rank, _ = mats.shape
    width = coef.shape[-1]
    where, shapes = {}, []
    for n, names in enumerate(outs):
        size = 0
        for c, rel in names:
            where[c, rel] = (n, size)
            size += len(chunks[c])
        shapes.append(jax.ShapeDtypeStruct((size, 2, per, rank, width), BF16))
    jobs = [[where[c, rel] + (rel, chunks[c]) for c, rel in group] for group in groups]
    slots = 2 * fam * len({base % planes for bases in chunks for base in bases})
    *found, table = pl.pallas_call(
        functools.partial(up_kernel, jobs),
        out_shape=shapes + [jax.ShapeDtypeStruct((per,) + table.shape[1:], BF16)],
        in_specs=[SMEM, SMEM, ANY, ANY, ANY],
        out_specs=[VMEM] * (len(outs) + 1),
        scratch_shapes=[
            pltpu.VMEM(coef.shape, BF16),
            pltpu.VMEM((slots, children, nz, per, 2, rank, rank), BF16),
            pltpu.SemaphoreType.DMA,
            pltpu.SemaphoreType.DMA((slots,)),
        ],
        compiler_params=PARAMS,
        cost_estimate=COST,
    )(at, dirs, *[pltpu.with_memory_space_constraint(x, pltpu.HBM) for x in (coef, mats, table)])
    return {name: (found[n], offset) for name, (n, offset) in where.items()}, found, table


def total_of(refs, offsets, count):
    total = None
    for ref, offset in zip(refs, offsets):
        term = ref[offset : offset + count].astype(F32)
        total = term if total is None else total + term
    return total.astype(BF16)


def add_kernel(offsets, *refs):
    refs[-1][...] = total_of(refs[:-1], offsets, refs[-1].shape[0])


def add(pieces, count):
    return pl.pallas_call(
        functools.partial(add_kernel, tuple(offset for _, offset in pieces)),
        out_shape=jax.ShapeDtypeStruct((count,) + pieces[0][0].shape[1:], BF16),
        in_specs=[VMEM] * len(pieces),
        out_specs=VMEM,
        compiler_params=PARAMS,
        cost_estimate=COST,
    )(*[array for array, _ in pieces])


def part_kernel(offsets, *refs):
    lists, outs = refs[:2], refs[2 + len(offsets) :]
    total = total_of(refs[2 : 2 + len(offsets)], offsets, len(outs))
    rows = total.shape[2] * total.shape[3]
    for n, out in enumerate(outs):
        for core in range(2):
            out[core, :rows] = total[n, core].reshape(rows, total.shape[4])
            out[core, rows:] = lists[core][...]


def part(pieces, count, lists):
    _, _, per, rank, width = pieces[0][0].shape
    return pl.pallas_call(
        functools.partial(part_kernel, tuple(offset for _, offset in pieces)),
        out_shape=[jax.ShapeDtypeStruct((2, per * rank + lists[0].shape[0], width), BF16)] * count,
        in_specs=[VMEM] * (2 + len(pieces)),
        out_specs=[VMEM] * count,
        compiler_params=PARAMS,
        cost_estimate=COST,
    )(*lists, *[array for array, _ in pieces])


def stack_kernel(core, *refs):
    for n, ref in enumerate(refs[:-1]):
        refs[-1][n] = ref[...] if core is None else ref[core]


def stack(arrays, core=None):
    shape = arrays[0].shape if core is None else arrays[0].shape[1:]
    return pl.pallas_call(
        functools.partial(stack_kernel, core),
        out_shape=jax.ShapeDtypeStruct((len(arrays),) + shape, arrays[0].dtype),
        in_specs=[VMEM] * len(arrays),
        out_specs=VMEM,
        compiler_params=PARAMS,
        cost_estimate=COST,
    )(*arrays)


def join_kernel(own_ref, other_ref, *outs):
    for n, out in enumerate(outs):
        out[0] = own_ref[n]
        out[1] = other_ref[n]


def join(own, other):
    return pl.pallas_call(
        join_kernel,
        out_shape=[jax.ShapeDtypeStruct((2,) + own.shape[1:], own.dtype)] * own.shape[0],
        in_specs=[VMEM] * 2,
        out_specs=[VMEM] * own.shape[0],
        compiler_params=PARAMS,
        cost_estimate=COST,
    )(own, other)


def couple_kernel(sizes, at_ref, table_ref, own_ref, *refs):
    planes, nz, most, held, chunks = sizes
    sources, (theirs_ref, mine_ref, wide, numbers, lists, sem) = refs[:-6], refs[-6:]
    me = lax.bitwise_and(at_ref[1], jnp.int32(1))
    per, _, _, rank, _ = table_ref.shape
    count = wide.shape[0] - 1
    held_by, pos = {}, 0
    for bases in chunks:
        for n, base in enumerate(bases):
            held_by[base] = (sources[pos + n].at[0], sources[pos + len(bases)].at[n])
        pos += len(bases) + 1
    gathered = sources[pos:]
    numbers[0] = own_ref[...].astype(F32).astype(jnp.int32)
    for z in range(1, nz):
        mine, theirs = (ref[per * rank :].astype(F32) for ref in held_by[z * planes])
        numbers[z] = jnp.where(me == 0, mine, theirs).astype(jnp.int32)
    copy = pltpu.make_async_copy(numbers, lists, sem)
    copy.start()
    parts = []
    if gathered:
        parts = [(t, gathered[0].at[t]) for t in range(gathered[0].shape[0])]
    else:
        for base, pair in held_by.items():
            for s, source in enumerate(pair):
                q = lax.bitwise_xor(xor(at_ref[0], base % planes), xor(me, s))
                parts.append((xor(at_ref[2], base // planes) * planes + q, source))
    for t, source in parts:
        for m in range(per):
            v = source[m * rank : (m + 1) * rank]
            wide[t, m, :rank] = v
            wide[t, m, rank:] = turned(v)
    wide[count] = jnp.zeros_like(wide[count])
    copy.wait()
    for row, s in ((theirs_ref, 1), (mine_ref, 0)):
        for n, base in enumerate(base for bases in chunks for base in bases):
            q, z = lax.bitwise_xor(xor(at_ref[0], base % planes), xor(me, s)), at_ref[2]
            for m in range(per):
                entry = (base // planes, q * held + z * per + m)
                active = lists[entry + (2 * most,)]
                total = None
                for k in range(most):
                    kind = lists[entry + (most + k,)]
                    source = jnp.where(k < active, lists[entry + (k,)], count)
                    both = jnp.concatenate([table_ref[m, kind, 0], table_ref[m, kind, 1]], axis=1)
                    term = dot(both, wide[source, m])
                    total = term if total is None else total + term
                row[n, m] = total.T.astype(BF16)


def couple(at, table, own, sources, sizes, total):
    per, _, _, rank, _ = table.shape
    width = sources[0].shape[-1]
    listed = (sizes[1],) + own.shape
    rows = sum(len(bases) for bases in sizes[-1])
    return pl.pallas_call(
        functools.partial(couple_kernel, sizes),
        out_shape=[jax.ShapeDtypeStruct((rows, per, width, rank), BF16)] * 2,
        in_specs=[SMEM] + [VMEM] * (2 + len(sources)),
        out_specs=[VMEM] * 2,
        scratch_shapes=[
            pltpu.VMEM((total + 1, per, 2 * rank, width), BF16),
            pltpu.VMEM(listed, jnp.int32),
            pltpu.SMEM(listed, jnp.int32),
            pltpu.SemaphoreType.DMA,
        ],
        compiler_params=PARAMS,
        cost_estimate=COST,
    )(at, table, own, *sources)


def down_kernel(jobs, last, at_ref, dir_ref, mat_ref, *rest):
    pieces = rest[: len(jobs)]
    if last:
        before, out_ref, sums = rest[len(jobs) :]
    else:
        (sums,) = rest[len(jobs) :]
    children, planes, fam, nz, per, _, rank, _ = mat_ref.shape
    sums[...] = jnp.zeros_like(sums)
    for piece, (rel, bases) in zip(pieces, jobs):
        for n, core in [(n, core) for n in range(len(bases)) for core in range(2)]:
            q, j, z = place(at_ref, planes, rel, bases[n], core)
            for m in range(per):
                e = ((q * fam + j) * nz + z) * per + m
                v = piece[n, core, m]
                x = jnp.concatenate([v, turned_rows(v)], axis=1)
                both = [mat_ref[c, q, j, z, m].reshape(2 * rank, rank) for c in range(children)]
                y = dot(x, jnp.concatenate(both, axis=1))
                for c in range(children):
                    sums[c, dir_ref[c, e]] += y[:, c * rank : (c + 1) * rank]
    if last:
        for c in range(children):
            for i in range(out_ref.shape[1]):
                out_ref[c, i] = (sums[c, i] + before[c, i]).T.astype(BF16)


def down(at, dirs, mats, jobs, pieces, groups, before=None):
    children, rank = mats.shape[0], mats.shape[-1]
    width = pieces[0].shape[-2]
    last = before is not None
    sums = (children, groups, width, rank)
    return pl.pallas_call(
        functools.partial(down_kernel, jobs, last),
        out_shape=jax.ShapeDtypeStruct((children, groups, rank, width), BF16) if last else jax.ShapeDtypeStruct(sums, F32),
        in_specs=[SMEM, SMEM] + [VMEM] * (1 + len(pieces) + (1 if last else 0)),
        out_specs=VMEM,
        scratch_shapes=[pltpu.VMEM(sums, F32)] if last else [],
        compiler_params=PARAMS,
        cost_estimate=COST,
    )(at, dirs, mats, *pieces, *([before] if last else []))


def body(nx, ny, child_coef, transfer, child_dir, couple_src, couple_kind, couple_count, couple_table):
    children, dirs, _, rank, _ = transfer.shape
    planes, held, most = couple_src.shape
    fam = ny // planes
    split = held % nx == 0
    nz = nx if split else 1
    per = held // nz
    partners = nz * planes
    at_y, at_x = lax.axis_index("gy"), lax.axis_index("gx")
    at = jnp.stack([at_y // fam, at_y % fam, at_x if split else jnp.zeros_like(at_x)]).astype(jnp.int32)
    mats = transfer.reshape(children, planes, fam, nz, per, 2, rank, rank)
    bases = tuple(range(partners - 2, -1, -2))
    half = len(bases) // 2
    chunks = tuple((base,) for base in bases[:half]) + (bases[half:],)

    def family(x, rel):
        return lax.ppermute(x, "gy", [(i, i ^ rel) for i in range(ny)])

    def partner(x, base):
        moves = [(r // planes) * ny + (r % planes) * fam for r in (base, base ^ 1)]
        axes, size = (("gx", "gy"), nx * ny) if split else ("gy", ny)
        return lax.ppermute(x, axes, [(i, i ^ moves[i & 1]) for i in range(size)])

    nearest = len(chunks) - 1
    order = range(len(chunks))
    top = fam - 1
    lead = [(c, top) for c in order[:-1]]
    rest = [(c, rel) for c in order for rel in range(1, fam, 2) if (c, rel) not in lead]
    keep = [(c, rel) for rel in range(fam - 2, -1, -2) for c in order]
    groups = [[(c, rel) for c in order] for rel in sorted(range(fam), key=lambda r: (-r, r))]
    sums, found, table = up(at, child_dir, child_coef, mats, couple_table, chunks, [lead, rest] + [[k] for k in keep], groups)
    got = {key: [sums[key]] for key in keep}
    for array, names in ((found[0], lead), (found[1], rest)):
        moved = family(array, 1)
        for c, rel in names:
            got[c, rel ^ 1].append((moved, sums[c, rel][1]))
    for bit in (1 << n for n in range(1, fam.bit_length() - 1)):
        for c in order:
            for rel in range(fam - 2, 0, -2):
                if rel & -rel == bit:
                    ready = add(got.pop((c, rel)), len(chunks[c]))
                    if bit == fam // 2:
                        ready, couple_src, couple_kind, couple_count = lax.optimization_barrier(
                            (ready, couple_src, couple_kind, couple_count)
                        )
                    moved = family(ready, bit)
                    got[c, rel ^ bit].append((moved, 0))
    lists = jnp.concatenate([couple_src, couple_kind, couple_count[..., None]], axis=-1).reshape(planes * held, -1)
    lists = jnp.pad(lists, ((0, -planes * held % 16), (0, rank - lists.shape[1]))).astype(BF16)
    both_lists = (lists, family(lists, 1))
    sources = []
    for c in order:
        arrived = [partner(x, base) for x, base in zip(part(got[c, 0], len(chunks[c]), both_lists), chunks[c])]
        sources += arrived + [family(stack(arrived, core=1), 1)]
    if not split:
        own = jnp.zeros((partners,) + sources[0].shape[1:], BF16)
        pos = 0
        for chunk in chunks:
            for n, base in enumerate(chunk):
                for s, value in enumerate((sources[pos + n][0], sources[pos + len(chunk)][n])):
                    spot = lax.bitwise_xor(at[0], jnp.int32(base ^ s)) ^ (at[1] & 1)
                    own = lax.dynamic_update_index_in_dim(own, value, spot, 0)
            pos += len(chunk) + 1
        sources.append(lax.all_gather(own, "gx", axis=0, tiled=True))
    theirs, mine = couple(at, table, lists, sources, (planes, nz, most, held, chunks), nx * planes)
    local = {base: partner(x, base) for base, x in zip(bases, join(mine, family(theirs, 1)))}

    groups = child_coef.shape[1]
    pieces = {(c, 0): stack([local[base] for base in chunks[c]]) for c in order}
    bits = [1 << n for n in range(fam.bit_length() - 2, -1, -1)]
    final = nearest - 1
    for c in [nearest] + list(order[:-1]):
        for bit in bits:
            for rel in sorted(r for g, r in pieces if g == c):
                if c != final or bit == fam // 2 or not rel & (fam // 2):
                    pieces[c, rel ^ bit] = family(pieces[c, rel], bit)
    last = [(final, rel) for rel in range(fam) if rel & (fam // 2)]
    soon = [key for key in pieces if key not in last]

    def work(keys):
        return tuple((rel, chunks[c]) for c, rel in keys)

    first = down(at, child_dir, mats, work(soon), [pieces[key] for key in soon], groups)
    pieces[last[0]], first = lax.optimization_barrier((pieces[last[0]], first))
    for bit in bits[1:]:
        for rel in sorted(r for g, r in pieces if g == final and r & (fam // 2)):
            pieces[final, rel ^ bit] = family(pieces[final, rel], bit)
    return down(at, child_dir, mats, work(last), [pieces[key] for key in last], groups, before=first)


def solution(mesh):
    return jax.shard_map(
        functools.partial(body, mesh.shape["gx"], mesh.shape["gy"]),
        mesh=mesh,
        in_specs=(
            P(("gx", "gy"), None, None, None),
            P(("gx", "gy"), None, None, None, None),
            P(("gx", "gy"), None),
            P("gx", "gy", None),
            P("gx", "gy", None),
            P("gx", "gy"),
            P("gy", None, None, None, None),
        ),
        out_specs=P(("gx", "gy"), None, None, None),
        check_vma=False,
    )
```

```python
import functools

import jax
import jax.numpy as jnp
from jax import lax
from jax.experimental import pallas as pl
from jax.experimental.pallas import tpu as pltpu
from jax.sharding import PartitionSpec as P

F32 = jnp.float32
BF16 = jnp.bfloat16
SMEM = pl.BlockSpec(memory_space=pltpu.SMEM)
VMEM = pl.BlockSpec(memory_space=pltpu.VMEM)
ANY = pl.BlockSpec(memory_space=pl.ANY)
COST = pl.CostEstimate(flops=10000000000, bytes_accessed=1000000, transcendentals=0)
PARAMS = pltpu.CompilerParams(vmem_limit_bytes=16 << 20)


def turned(v):
    half = v.shape[-1] // 2
    return jnp.concatenate([-v[..., half:], v[..., :half]], axis=-1)


def turned_rows(v):
    half = v.shape[0] // 2
    return jnp.concatenate([-v[half:], v[:half]], axis=0)


def dot(a, b):
    return jnp.dot(a, b, preferred_element_type=F32)


def xor(a, b):
    return lax.bitwise_xor(a, jnp.int32(b))


def place(at_ref, planes, rel, base, core):
    turn = lax.bitwise_and(xor(at_ref[1], rel), jnp.int32(1))
    q = lax.bitwise_xor(xor(at_ref[0], base % planes), turn)
    return q, xor(at_ref[1], rel ^ core), xor(at_ref[2], base // planes)


def up_kernel(groups, at_ref, dir_hbm, coef_hbm, mat_hbm, table_hbm, *rest):
    outs, (dir_ref, coef_ref, mat_ref, dir_sem, coef_sem, mat_sem) = rest[:-6], rest[-6:]
    children, planes, fam, nz, per = mat_hbm.shape[:5]

    coef_copy = pltpu.make_async_copy(coef_hbm, coef_ref, coef_sem)
    coef_copy.start()
    dir_copy = pltpu.make_async_copy(dir_hbm, dir_ref, dir_sem)
    dir_copy.start()
    slots, flying = {}, []

    def start(group):
        copies = []
        for _, _, rel, bases in group:
            for base, core in [(base, core) for base in bases for core in range(2)]:
                key = (rel, core, base % planes)
                if key not in slots:
                    slots[key] = slot = len(slots)
                    q, j, _ = place(at_ref, planes, rel, base, core)
                    copies.append(pltpu.make_async_copy(mat_hbm.at[:, q, j], mat_ref.at[slot], mat_sem.at[slot]))
                    copies[-1].start()
        flying.append(copies)

    for group in groups[:2]:
        start(group)
    coef_copy.wait()
    dir_copy.wait()
    for number, group in enumerate(groups):
        for copy in flying[number]:
            copy.wait()
        if number + 2 < len(groups):
            start(groups[number + 2])
        elif number + 2 == len(groups):
            table_copy = pltpu.make_async_copy(table_hbm.at[pl.ds(at_ref[2] * per, per)], outs[-1], coef_sem)
            table_copy.start()
        for out, offset, rel, bases in group:
            for n, core in [(n, core) for n in range(len(bases)) for core in range(2)]:
                q, j, z = place(at_ref, planes, rel, bases[n], core)
                slot = slots[rel, core, bases[n] % planes]
                for m in range(per):
                    left, right = [], []
                    for c in range(children):
                        v = coef_ref[c, dir_ref[c, ((q * fam + j) * nz + z) * per + m]]
                        left += [mat_ref[slot, c, z, m, 0], mat_ref[slot, c, z, m, 1]]
                        right += [v, turned(v)]
                    total = dot(jnp.concatenate(left, axis=1), jnp.concatenate(right, axis=0))
                    outs[out][offset + n, core, m] = total.astype(BF16)
    table_copy.wait()


def up(at, dirs, coef, mats, table, chunks, outs, groups):
    children, planes, fam, nz, per, _, rank, _ = mats.shape
    width = coef.shape[-1]
    where, shapes = {}, []
    for n, names in enumerate(outs):
        size = 0
        for c, rel in names:
            where[c, rel] = (n, size)
            size += len(chunks[c])
        shapes.append(jax.ShapeDtypeStruct((size, 2, per, rank, width), BF16))
    jobs = [[where[c, rel] + (rel, chunks[c]) for c, rel in group] for group in groups]
    slots = 2 * fam * len({base % planes for bases in chunks for base in bases})
    *found, table = pl.pallas_call(
        functools.partial(up_kernel, jobs),
        out_shape=shapes + [jax.ShapeDtypeStruct((per,) + table.shape[1:], BF16)],
        in_specs=[SMEM, ANY, ANY, ANY, ANY],
        out_specs=[VMEM] * (len(outs) + 1),
        scratch_shapes=[
            pltpu.SMEM(dirs.shape, jnp.int32),
            pltpu.VMEM(coef.shape, BF16),
            pltpu.VMEM((slots, children, nz, per, 2, rank, rank), BF16),
            pltpu.SemaphoreType.DMA,
            pltpu.SemaphoreType.DMA,
            pltpu.SemaphoreType.DMA((slots,)),
        ],
        compiler_params=PARAMS,
        cost_estimate=COST,
    )(at, *[pltpu.with_memory_space_constraint(x, pltpu.HBM) for x in (dirs, coef, mats, table)])
    return {name: (found[n], offset) for name, (n, offset) in where.items()}, found, table


def total_of(refs, offsets, count):
    total = None
    for ref, offset in zip(refs, offsets):
        term = ref[offset : offset + count].astype(F32)
        total = term if total is None else total + term
    return total.astype(BF16)


def add_kernel(offsets, *refs):
    refs[-1][...] = total_of(refs[:-1], offsets, refs[-1].shape[0])


def add(pieces, count):
    return pl.pallas_call(
        functools.partial(add_kernel, tuple(offset for _, offset in pieces)),
        out_shape=jax.ShapeDtypeStruct((count,) + pieces[0][0].shape[1:], BF16),
        in_specs=[VMEM] * len(pieces),
        out_specs=VMEM,
        compiler_params=PARAMS,
        cost_estimate=COST,
    )(*[array for array, _ in pieces])


def part_kernel(offsets, *refs):
    lists, outs = refs[:2], refs[2 + len(offsets) :]
    total = total_of(refs[2 : 2 + len(offsets)], offsets, len(outs))
    rows = total.shape[2] * total.shape[3]
    for n, out in enumerate(outs):
        for core in range(2):
            out[core, :rows] = total[n, core].reshape(rows, total.shape[4])
            out[core, rows:] = lists[core][...]


def part(pieces, count, lists):
    _, _, per, rank, width = pieces[0][0].shape
    return pl.pallas_call(
        functools.partial(part_kernel, tuple(offset for _, offset in pieces)),
        out_shape=[jax.ShapeDtypeStruct((2, per * rank + lists[0].shape[0], width), BF16)] * count,
        in_specs=[VMEM] * (2 + len(pieces)),
        out_specs=[VMEM] * count,
        compiler_params=PARAMS,
        cost_estimate=COST,
    )(*lists, *[array for array, _ in pieces])


def stack_kernel(core, *refs):
    for n, ref in enumerate(refs[:-1]):
        refs[-1][n] = ref[...] if core is None else ref[core]


def stack(arrays, core=None):
    shape = arrays[0].shape if core is None else arrays[0].shape[1:]
    return pl.pallas_call(
        functools.partial(stack_kernel, core),
        out_shape=jax.ShapeDtypeStruct((len(arrays),) + shape, arrays[0].dtype),
        in_specs=[VMEM] * len(arrays),
        out_specs=VMEM,
        compiler_params=PARAMS,
        cost_estimate=COST,
    )(*arrays)


def join_kernel(own_ref, other_ref, *outs):
    for n, out in enumerate(outs):
        out[0] = own_ref[n]
        out[1] = other_ref[n]


def join(own, other):
    return pl.pallas_call(
        join_kernel,
        out_shape=[jax.ShapeDtypeStruct((2,) + own.shape[1:], own.dtype)] * own.shape[0],
        in_specs=[VMEM] * 2,
        out_specs=[VMEM] * own.shape[0],
        compiler_params=PARAMS,
        cost_estimate=COST,
    )(own, other)


def couple_kernel(sizes, at_ref, table_ref, own_ref, *refs):
    planes, nz, most, held, chunks, bases = sizes
    sources, (theirs_ref, mine_ref, wide, numbers, lists, sem) = refs[:-6], refs[-6:]
    me = lax.bitwise_and(at_ref[1], jnp.int32(1))
    per, _, _, rank, _ = table_ref.shape
    count = wide.shape[0] - 1
    held_by, pos = {}, 0
    for chunk in chunks:
        for n, base in enumerate(chunk):
            held_by[base] = (sources[pos + n].at[0], sources[pos + len(chunk)].at[n])
        pos += len(chunk) + 1
    gathered = sources[pos:]
    numbers[0] = own_ref[...].astype(F32).astype(jnp.int32)
    for z in range(1, nz):
        mine, theirs = (ref[per * rank :].astype(F32) for ref in held_by[z * planes])
        numbers[z] = jnp.where(me == 0, mine, theirs).astype(jnp.int32)
    copy = pltpu.make_async_copy(numbers, lists, sem)
    copy.start()
    parts = []
    if gathered:
        parts = [(t, gathered[0].at[t]) for t in range(gathered[0].shape[0])]
    else:
        for base, pair in held_by.items():
            for s, source in enumerate(pair):
                q = lax.bitwise_xor(xor(at_ref[0], base % planes), xor(me, s))
                parts.append((xor(at_ref[2], base // planes) * planes + q, source))
    for t, source in parts:
        for m in range(per):
            v = source[m * rank : (m + 1) * rank]
            wide[t, m, :rank] = v
            wide[t, m, rank:] = turned(v)
    wide[count] = jnp.zeros_like(wide[count])
    copy.wait()
    for row, s in ((theirs_ref, 1), (mine_ref, 0)):
        for n, base in enumerate(bases):
            q, z = lax.bitwise_xor(xor(at_ref[0], base % planes), xor(me, s)), at_ref[2]
            for m in range(per):
                entry = (base // planes, q * held + z * per + m)
                active = lists[entry + (2 * most,)]
                total = None
                for k in range(most):
                    kind = lists[entry + (most + k,)]
                    source = jnp.where(k < active, lists[entry + (k,)], count)
                    both = jnp.concatenate([table_ref[m, kind, 0], table_ref[m, kind, 1]], axis=1)
                    term = dot(both, wide[source, m])
                    total = term if total is None else total + term
                row[n, m] = total.T.astype(BF16)


def couple(at, table, own, sources, sizes, total):
    per, _, _, rank, _ = table.shape
    width = sources[0].shape[-1]
    listed = (sizes[1],) + own.shape
    rows = len(sizes[-1])
    return pl.pallas_call(
        functools.partial(couple_kernel, sizes),
        out_shape=[jax.ShapeDtypeStruct((rows, per, width, rank), BF16)] * 2,
        in_specs=[SMEM] + [VMEM] * (2 + len(sources)),
        out_specs=[VMEM] * 2,
        scratch_shapes=[
            pltpu.VMEM((total + 1, per, 2 * rank, width), BF16),
            pltpu.VMEM(listed, jnp.int32),
            pltpu.SMEM(listed, jnp.int32),
            pltpu.SemaphoreType.DMA,
        ],
        compiler_params=PARAMS,
        cost_estimate=COST,
    )(at, table, own, *sources)


def down_kernel(jobs, last, at_ref, dir_ref, mat_ref, *rest):
    pieces = rest[: len(jobs)]
    if last:
        before, out_ref, sums, staged, sems = rest[len(jobs) :]
    else:
        (sums,) = rest[len(jobs) :]
    children, planes, fam, nz, per, _, rank, _ = mat_ref.shape
    sums[...] = jnp.zeros_like(sums)
    for piece, (rel, bases) in zip(pieces, jobs):
        for n, core in [(n, core) for n in range(len(bases)) for core in range(2)]:
            q, j, z = place(at_ref, planes, rel, bases[n], core)
            for m in range(per):
                e = ((q * fam + j) * nz + z) * per + m
                v = piece[n, core, m]
                x = jnp.concatenate([v, turned_rows(v)], axis=1)
                both = [mat_ref[c, q, j, z, m].reshape(2 * rank, rank) for c in range(children)]
                y = dot(x, jnp.concatenate(both, axis=1))
                for c in range(children):
                    sums[c, dir_ref[c, e]] += y[:, c * rank : (c + 1) * rank]
    if last:
        copies = []
        for c in range(children):
            for i in range(staged.shape[1]):
                staged[c, i] = (sums[c, i] + before[c, i]).T.astype(BF16)
            copies.append(pltpu.make_async_copy(staged.at[c], out_ref.at[c], sems.at[c]))
            copies[-1].start()
        for copy in copies:
            copy.wait()


def down(at, dirs, mats, jobs, pieces, groups, before=None):
    children, rank = mats.shape[0], mats.shape[-1]
    width = pieces[0].shape[-2]
    last = before is not None
    sums = (children, groups, width, rank)
    return pl.pallas_call(
        functools.partial(down_kernel, jobs, last),
        out_shape=jax.ShapeDtypeStruct((children, groups, rank, width), BF16) if last else jax.ShapeDtypeStruct(sums, F32),
        in_specs=[SMEM, SMEM] + [VMEM] * (1 + len(pieces) + (1 if last else 0)),
        out_specs=ANY if last else VMEM,
        scratch_shapes=[
            pltpu.VMEM(sums, F32),
            pltpu.VMEM((children, groups, rank, width), BF16),
            pltpu.SemaphoreType.DMA((children,)),
        ]
        if last
        else [],
        compiler_params=PARAMS,
        cost_estimate=COST,
    )(at, dirs, mats, *pieces, *([before] if last else []))


def body(nx, ny, child_coef, transfer, child_dir, couple_src, couple_kind, couple_count, couple_table):
    children, dirs, _, rank, _ = transfer.shape
    planes, held, most = couple_src.shape
    fam = ny // planes
    split = held % nx == 0
    nz = nx if split else 1
    per = held // nz
    partners = nz * planes
    at_y, at_x = lax.axis_index("gy"), lax.axis_index("gx")
    at = jnp.stack([at_y // fam, at_y % fam, at_x if split else jnp.zeros_like(at_x)]).astype(jnp.int32)
    mats = transfer.reshape(children, planes, fam, nz, per, 2, rank, rank)
    bases = tuple(range(partners - 2, -1, -2))
    half = len(bases) // 2
    chunks = tuple((base,) for pair in zip(bases[:half], bases[half:]) for base in pair)

    def family(x, rel):
        return lax.ppermute(x, "gy", [(i, i ^ rel) for i in range(ny)])

    def partner(x, base):
        moves = [(r // planes) * ny + (r % planes) * fam for r in (base, base ^ 1)]
        axes, size = (("gx", "gy"), nx * ny) if split else ("gy", ny)
        return lax.ppermute(x, axes, [(i, i ^ moves[i & 1]) for i in range(size)])

    nearest = len(chunks) - 1
    order = range(len(chunks))
    top = fam - 1
    lead = [(c, top) for c in order[:-1]]
    rest = [(c, rel) for c in order for rel in range(1, fam, 2) if (c, rel) not in lead]
    keep = [(c, rel) for rel in range(fam - 2, -1, -2) for c in order]
    groups = [[(c, rel) for c in order] for rel in sorted(range(fam), key=lambda r: (-r, r))]
    sums, found, table = up(at, child_dir, child_coef, mats, couple_table, chunks, [lead, rest] + [[k] for k in keep], groups)
    got = {key: [sums[key]] for key in keep}
    for array, names in ((found[0], lead), (found[1], rest)):
        moved = family(array, 1)
        for c, rel in names:
            got[c, rel ^ 1].append((moved, sums[c, rel][1]))
    for bit in (1 << n for n in range(1, fam.bit_length() - 1)):
        for c in order:
            for rel in range(fam - 2, 0, -2):
                if rel & -rel == bit:
                    ready = add(got.pop((c, rel)), len(chunks[c]))
                    if bit == fam // 2:
                        ready, couple_src, couple_kind, couple_count = lax.optimization_barrier(
                            (ready, couple_src, couple_kind, couple_count)
                        )
                    moved = family(ready, bit)
                    got[c, rel ^ bit].append((moved, 0))
    lists = jnp.concatenate([couple_src, couple_kind, couple_count[..., None]], axis=-1).reshape(planes * held, -1)
    lists = jnp.pad(lists, ((0, -planes * held % 16), (0, rank - lists.shape[1]))).astype(BF16)
    both_lists = (lists, family(lists, 1))
    sources = []
    for c in order:
        arrived = [partner(x, base) for x, base in zip(part(got[c, 0], len(chunks[c]), both_lists), chunks[c])]
        sources += arrived + [family(stack(arrived, core=1), 1)]
    if not split:
        own = jnp.zeros((partners,) + sources[0].shape[1:], BF16)
        pos = 0
        for chunk in chunks:
            for n, base in enumerate(chunk):
                for s, value in enumerate((sources[pos + n][0], sources[pos + len(chunk)][n])):
                    spot = lax.bitwise_xor(at[0], jnp.int32(base ^ s)) ^ (at[1] & 1)
                    own = lax.dynamic_update_index_in_dim(own, value, spot, 0)
            pos += len(chunk) + 1
        sources.append(lax.all_gather(own, "gx", axis=0, tiled=True))
    theirs, mine = couple(at, table, lists, sources, (planes, nz, most, held, chunks, bases), nx * planes)
    local = {base: partner(x, base) for base, x in zip(bases, join(mine, family(theirs, 1)))}

    groups = child_coef.shape[1]
    chunks = tuple((base,) for base in bases[:half]) + (bases[half:],)
    order = range(len(chunks))
    nearest = len(chunks) - 1
    pieces = {(c, 0): stack([local[base] for base in chunks[c]]) for c in order}
    bits = [1 << n for n in range(fam.bit_length() - 2, -1, -1)]
    final = nearest - 1
    for c in [nearest] + list(order[:-1]):
        for bit in bits:
            for rel in sorted(r for g, r in pieces if g == c):
                if c != final or bit == fam // 2 or not rel & (fam // 2):
                    pieces[c, rel ^ bit] = family(pieces[c, rel], bit)
    last = [(final, rel) for rel in range(fam) if rel & (fam // 2)]
    soon = [key for key in pieces if key not in last]

    def work(keys):
        return tuple((rel, chunks[c]) for c, rel in keys)

    first = down(at, child_dir, mats, work(soon), [pieces[key] for key in soon], groups)
    pieces[last[0]], first = lax.optimization_barrier((pieces[last[0]], first))
    for bit in bits[1:]:
        for rel in sorted(r for g, r in pieces if g == final and r & (fam // 2)):
            pieces[final, rel ^ bit] = family(pieces[final, rel], bit)
    return down(at, child_dir, mats, work(last), [pieces[key] for key in last], groups, before=first)


def solution(mesh):
    return jax.shard_map(
        functools.partial(body, mesh.shape["gx"], mesh.shape["gy"]),
        mesh=mesh,
        in_specs=(
            P(("gx", "gy"), None, None, None),
            P(("gx", "gy"), None, None, None, None),
            P(("gx", "gy"), None),
            P("gx", "gy", None),
            P("gx", "gy", None),
            P("gx", "gy"),
            P("gy", None, None, None, None),
        ),
        out_specs=P(("gx", "gy"), None, None, None),
        check_vma=False,
    )
```

```python
import functools

import jax
import jax.numpy as jnp
from jax import lax
from jax.experimental import pallas as pl
from jax.experimental.pallas import tpu as pltpu
from jax.sharding import PartitionSpec as P

F32 = jnp.float32
BF16 = jnp.bfloat16
SMEM = pl.BlockSpec(memory_space=pltpu.SMEM)
VMEM = pl.BlockSpec(memory_space=pltpu.VMEM)
ANY = pl.BlockSpec(memory_space=pl.ANY)
COST = pl.CostEstimate(flops=10000000000, bytes_accessed=1000000, transcendentals=0)
PARAMS = pltpu.CompilerParams(vmem_limit_bytes=16 << 20)


def turned(v):
    half = v.shape[-1] // 2
    return jnp.concatenate([-v[..., half:], v[..., :half]], axis=-1)


def turned_rows(v):
    half = v.shape[0] // 2
    return jnp.concatenate([-v[half:], v[:half]], axis=0)


def dot(a, b):
    return jnp.dot(a, b, preferred_element_type=F32)


def xor(a, b):
    return lax.bitwise_xor(a, jnp.int32(b))


def place(at_ref, planes, rel, base, core):
    turn = lax.bitwise_and(xor(at_ref[1], rel), jnp.int32(1))
    q = lax.bitwise_xor(xor(at_ref[0], base % planes), turn)
    return q, xor(at_ref[1], rel ^ core), xor(at_ref[2], base // planes)


def up_kernel(groups, at_ref, dir_hbm, coef_hbm, mat_hbm, table_hbm, *rest):
    outs, (dir_ref, coef_ref, mat_ref, dir_sem, coef_sem, mat_sem) = rest[:-6], rest[-6:]
    children, planes, fam, nz, per = mat_hbm.shape[:5]

    coef_copy = pltpu.make_async_copy(coef_hbm, coef_ref, coef_sem)
    coef_copy.start()
    dir_copy = pltpu.make_async_copy(dir_hbm, dir_ref, dir_sem)
    dir_copy.start()
    slots, flying = {}, []

    def start(group):
        copies = []
        for _, _, rel, bases in group:
            for base, core in [(base, core) for base in bases for core in range(2)]:
                key = (rel, core, base % planes)
                if key not in slots:
                    slots[key] = slot = len(slots)
                    q, j, _ = place(at_ref, planes, rel, base, core)
                    copies.append(pltpu.make_async_copy(mat_hbm.at[:, q, j], mat_ref.at[slot], mat_sem.at[slot]))
                    copies[-1].start()
        flying.append(copies)

    for group in groups[:2]:
        start(group)
    coef_copy.wait()
    dir_copy.wait()
    for number, group in enumerate(groups):
        for copy in flying[number]:
            copy.wait()
        if number + 2 < len(groups):
            start(groups[number + 2])
        elif number + 2 == len(groups):
            table_copy = pltpu.make_async_copy(table_hbm.at[pl.ds(at_ref[2] * per, per)], outs[-1], coef_sem)
            table_copy.start()
        for out, offset, rel, bases in group:
            for n, core in [(n, core) for n in range(len(bases)) for core in range(2)]:
                q, j, z = place(at_ref, planes, rel, bases[n], core)
                slot = slots[rel, core, bases[n] % planes]
                for m in range(per):
                    left, right = [], []
                    for c in range(children):
                        v = coef_ref[c, dir_ref[c, ((q * fam + j) * nz + z) * per + m]]
                        left += [mat_ref[slot, c, z, m, 0], mat_ref[slot, c, z, m, 1]]
                        right += [v, turned(v)]
                    total = dot(jnp.concatenate(left, axis=1), jnp.concatenate(right, axis=0))
                    outs[out][offset + n, core, m] = total.astype(BF16)
    table_copy.wait()


def up(at, dirs, coef, mats, table, chunks, outs, groups):
    children, planes, fam, nz, per, _, rank, _ = mats.shape
    width = coef.shape[-1]
    where, shapes = {}, []
    for n, names in enumerate(outs):
        size = 0
        for c, rel in names:
            where[c, rel] = (n, size)
            size += len(chunks[c])
        shapes.append(jax.ShapeDtypeStruct((size, 2, per, rank, width), BF16))
    jobs = [[where[c, rel] + (rel, chunks[c]) for c, rel in group] for group in groups]
    slots = 2 * fam * len({base % planes for bases in chunks for base in bases})
    *found, table = pl.pallas_call(
        functools.partial(up_kernel, jobs),
        out_shape=shapes + [jax.ShapeDtypeStruct((per,) + table.shape[1:], BF16)],
        in_specs=[SMEM, ANY, ANY, ANY, ANY],
        out_specs=[VMEM] * (len(outs) + 1),
        scratch_shapes=[
            pltpu.SMEM(dirs.shape, jnp.int32),
            pltpu.VMEM(coef.shape, BF16),
            pltpu.VMEM((slots, children, nz, per, 2, rank, rank), BF16),
            pltpu.SemaphoreType.DMA,
            pltpu.SemaphoreType.DMA,
            pltpu.SemaphoreType.DMA((slots,)),
        ],
        compiler_params=PARAMS,
        cost_estimate=COST,
    )(at, *[pltpu.with_memory_space_constraint(x, pltpu.HBM) for x in (dirs, coef, mats, table)])
    return {name: (found[n], offset) for name, (n, offset) in where.items()}, found, table


def total_of(refs, offsets, count):
    total = None
    for ref, offset in zip(refs, offsets):
        term = ref[offset : offset + count].astype(F32)
        total = term if total is None else total + term
    return total.astype(BF16)


def add_kernel(offsets, *refs):
    refs[-1][...] = total_of(refs[:-1], offsets, refs[-1].shape[0])


def add(pieces, count):
    return pl.pallas_call(
        functools.partial(add_kernel, tuple(offset for _, offset in pieces)),
        out_shape=jax.ShapeDtypeStruct((count,) + pieces[0][0].shape[1:], BF16),
        in_specs=[VMEM] * len(pieces),
        out_specs=VMEM,
        compiler_params=PARAMS,
        cost_estimate=COST,
    )(*[array for array, _ in pieces])


def part_kernel(offsets, *refs):
    lists, outs = refs[:2], refs[2 + len(offsets) :]
    total = total_of(refs[2 : 2 + len(offsets)], offsets, len(outs))
    rows = total.shape[2] * total.shape[3]
    for n, out in enumerate(outs):
        for core in range(2):
            out[core, :rows] = total[n, core].reshape(rows, total.shape[4])
            out[core, rows:] = lists[core][...]


def part(pieces, count, lists):
    _, _, per, rank, width = pieces[0][0].shape
    return pl.pallas_call(
        functools.partial(part_kernel, tuple(offset for _, offset in pieces)),
        out_shape=[jax.ShapeDtypeStruct((2, per * rank + lists[0].shape[0], width), BF16)] * count,
        in_specs=[VMEM] * (2 + len(pieces)),
        out_specs=[VMEM] * count,
        compiler_params=PARAMS,
        cost_estimate=COST,
    )(*lists, *[array for array, _ in pieces])


def stack_kernel(core, *refs):
    for n, ref in enumerate(refs[:-1]):
        refs[-1][n] = ref[...] if core is None else ref[core]


def stack(arrays, core=None):
    shape = arrays[0].shape if core is None else arrays[0].shape[1:]
    return pl.pallas_call(
        functools.partial(stack_kernel, core),
        out_shape=jax.ShapeDtypeStruct((len(arrays),) + shape, arrays[0].dtype),
        in_specs=[VMEM] * len(arrays),
        out_specs=VMEM,
        compiler_params=PARAMS,
        cost_estimate=COST,
    )(*arrays)


def join_kernel(own_ref, other_ref, *outs):
    for n, out in enumerate(outs):
        out[0] = own_ref[n]
        out[1] = other_ref[n]


def join(own, other):
    return pl.pallas_call(
        join_kernel,
        out_shape=[jax.ShapeDtypeStruct((2,) + own.shape[1:], own.dtype)] * own.shape[0],
        in_specs=[VMEM] * 2,
        out_specs=[VMEM] * own.shape[0],
        compiler_params=PARAMS,
        cost_estimate=COST,
    )(own, other)


def couple_kernel(sizes, at_ref, table_ref, own_ref, *refs):
    planes, nz, most, held, chunks, bases = sizes
    sources, (theirs_ref, mine_ref, wide, numbers, lists, sem) = refs[:-6], refs[-6:]
    me = lax.bitwise_and(at_ref[1], jnp.int32(1))
    per, _, _, rank, _ = table_ref.shape
    count = wide.shape[0] - 1
    held_by, pos = {}, 0
    for chunk in chunks:
        for n, base in enumerate(chunk):
            held_by[base] = (sources[pos + n].at[0], sources[pos + len(chunk)].at[n])
        pos += len(chunk) + 1
    gathered = sources[pos:]
    for z in range(nz):
        if z == 0:
            tile = own_ref[...].astype(F32)
        else:
            mine, theirs = (ref[per * rank :].astype(F32) for ref in held_by[z * planes])
            tile = jnp.where(me == 0, mine, theirs)
        row_of = lax.broadcasted_iota(jnp.int32, tile.shape, 0)
        for q in range(planes):
            row = jnp.where(row_of == at_ref[2] * planes + q, tile, 0.0)
            numbers[pl.ds(z * planes + q, 1)] = jnp.sum(row, axis=0, keepdims=True).astype(jnp.int32)
    copy = pltpu.make_async_copy(numbers, lists, sem)
    copy.start()
    parts = []
    if gathered:
        parts = [(t, gathered[0].at[t]) for t in range(gathered[0].shape[0])]
    else:
        for base, pair in held_by.items():
            for s, source in enumerate(pair):
                q = lax.bitwise_xor(xor(at_ref[0], base % planes), xor(me, s))
                parts.append((xor(at_ref[2], base // planes) * planes + q, source))
    for t, source in parts:
        for m in range(per):
            v = source[m * rank : (m + 1) * rank]
            wide[t, m, :rank] = v
            wide[t, m, rank:] = turned(v)
    wide[count] = jnp.zeros_like(wide[count])
    copy.wait()
    for row, s in ((theirs_ref, 1), (mine_ref, 0)):
        for n, base in enumerate(bases):
            q = lax.bitwise_xor(xor(at_ref[0], base % planes), xor(me, s))
            for m in range(per):
                line, column = base // planes * planes + q, m * (2 * most + 1)
                active = lists[line, column + 2 * most]
                total = None
                for k in range(most):
                    kind = lists[line, column + most + k]
                    source = jnp.where(k < active, lists[line, column + k], count)
                    both = jnp.concatenate([table_ref[m, kind, 0], table_ref[m, kind, 1]], axis=1)
                    term = dot(both, wide[source, m])
                    total = term if total is None else total + term
                row[n, m] = total.T.astype(BF16)


def couple(at, table, own, sources, sizes, total):
    per, _, _, rank, _ = table.shape
    width = sources[0].shape[-1]
    listed = (sizes[0] * sizes[1], own.shape[1])
    rows = len(sizes[-1])
    return pl.pallas_call(
        functools.partial(couple_kernel, sizes),
        out_shape=[jax.ShapeDtypeStruct((rows, per, width, rank), BF16)] * 2,
        in_specs=[SMEM] + [VMEM] * (2 + len(sources)),
        out_specs=[VMEM] * 2,
        scratch_shapes=[
            pltpu.VMEM((total + 1, per, 2 * rank, width), BF16),
            pltpu.VMEM(listed, jnp.int32),
            pltpu.SMEM(listed, jnp.int32),
            pltpu.SemaphoreType.DMA,
        ],
        compiler_params=PARAMS,
        cost_estimate=COST,
    )(at, table, own, *sources)


def down_kernel(jobs, last, at_ref, dir_ref, mat_ref, *rest):
    pieces = rest[: len(jobs)]
    if last:
        before, out_ref, sums, staged, sems = rest[len(jobs) :]
    else:
        (sums,) = rest[len(jobs) :]
    children, planes, fam, nz, per, _, rank, _ = mat_ref.shape
    sums[...] = jnp.zeros_like(sums)
    for piece, (rel, bases) in zip(pieces, jobs):
        for n, core in [(n, core) for n in range(len(bases)) for core in range(2)]:
            q, j, z = place(at_ref, planes, rel, bases[n], core)
            for m in range(per):
                e = ((q * fam + j) * nz + z) * per + m
                v = piece[n, core, m]
                x = jnp.concatenate([v, turned_rows(v)], axis=1)
                both = [mat_ref[c, q, j, z, m].reshape(2 * rank, rank) for c in range(children)]
                y = dot(x, jnp.concatenate(both, axis=1))
                for c in range(children):
                    sums[c, dir_ref[c, e]] += y[:, c * rank : (c + 1) * rank]
    if last:
        copies = []
        for c in range(children):
            for i in range(staged.shape[1]):
                staged[c, i] = (sums[c, i] + before[c, i]).T.astype(BF16)
            copies.append(pltpu.make_async_copy(staged.at[c], out_ref.at[c], sems.at[c]))
            copies[-1].start()
        for copy in copies:
            copy.wait()


def down(at, dirs, mats, jobs, pieces, groups, before=None):
    children, rank = mats.shape[0], mats.shape[-1]
    width = pieces[0].shape[-2]
    last = before is not None
    sums = (children, groups, width, rank)
    return pl.pallas_call(
        functools.partial(down_kernel, jobs, last),
        out_shape=jax.ShapeDtypeStruct((children, groups, rank, width), BF16) if last else jax.ShapeDtypeStruct(sums, F32),
        in_specs=[SMEM, SMEM] + [VMEM] * (1 + len(pieces) + (1 if last else 0)),
        out_specs=ANY if last else VMEM,
        scratch_shapes=[
            pltpu.VMEM(sums, F32),
            pltpu.VMEM((children, groups, rank, width), BF16),
            pltpu.SemaphoreType.DMA((children,)),
        ]
        if last
        else [],
        compiler_params=PARAMS,
        cost_estimate=COST,
    )(at, dirs, mats, *pieces, *([before] if last else []))


def body(nx, ny, child_coef, transfer, child_dir, couple_src, couple_kind, couple_count, couple_table):
    children, dirs, _, rank, _ = transfer.shape
    planes, held, most = couple_src.shape
    fam = ny // planes
    split = held % nx == 0
    nz = nx if split else 1
    per = held // nz
    partners = nz * planes
    at_y, at_x = lax.axis_index("gy"), lax.axis_index("gx")
    at = jnp.stack([at_y // fam, at_y % fam, at_x if split else jnp.zeros_like(at_x)]).astype(jnp.int32)
    mats = transfer.reshape(children, planes, fam, nz, per, 2, rank, rank)
    bases = tuple(range(partners - 2, -1, -2))
    half = len(bases) // 2
    chunks = tuple((base,) for pair in zip(bases[:half], bases[half:]) for base in pair)

    def family(x, rel):
        return lax.ppermute(x, "gy", [(i, i ^ rel) for i in range(ny)])

    def partner(x, base):
        moves = [(r // planes) * ny + (r % planes) * fam for r in (base, base ^ 1)]
        axes, size = (("gx", "gy"), nx * ny) if split else ("gy", ny)
        return lax.ppermute(x, axes, [(i, i ^ moves[i & 1]) for i in range(size)])

    nearest = len(chunks) - 1
    order = range(len(chunks))
    top = fam - 1
    lead = [(c, top) for c in order[:-1]]
    rest = [(c, rel) for c in order for rel in range(1, fam, 2) if (c, rel) not in lead]
    keep = [(c, rel) for rel in range(fam - 2, -1, -2) for c in order]
    groups = [[(c, rel) for c in order] for rel in sorted(range(fam), key=lambda r: (-r, r))]
    sums, found, table = up(at, child_dir, child_coef, mats, couple_table, chunks, [lead, rest] + [[k] for k in keep], groups)
    got = {key: [sums[key]] for key in keep}
    for array, names in ((found[0], lead), (found[1], rest)):
        moved = family(array, 1)
        for c, rel in names:
            got[c, rel ^ 1].append((moved, sums[c, rel][1]))
    for bit in (1 << n for n in range(1, fam.bit_length() - 1)):
        for c in order:
            for rel in range(fam - 2, 0, -2):
                if rel & -rel == bit:
                    ready = add(got.pop((c, rel)), len(chunks[c]))
                    if bit == fam // 2:
                        ready, couple_src, couple_kind, couple_count = lax.optimization_barrier(
                            (ready, couple_src, couple_kind, couple_count)
                        )
                    moved = family(ready, bit)
                    got[c, rel ^ bit].append((moved, 0))
    lists = jnp.concatenate([couple_src, couple_kind, couple_count[..., None]], axis=-1)
    lists = lists.reshape(planes, nz, -1).transpose(1, 0, 2).reshape(partners, -1)
    lists = jnp.pad(lists, ((0, -partners % 16), (0, rank - lists.shape[1]))).astype(BF16)
    both_lists = (lists, family(lists, 1))
    sources = []
    for c in order:
        arrived = [partner(x, base) for x, base in zip(part(got[c, 0], len(chunks[c]), both_lists), chunks[c])]
        sources += arrived + [family(stack(arrived, core=1), 1)]
    if not split:
        own = jnp.zeros((partners,) + sources[0].shape[1:], BF16)
        pos = 0
        for chunk in chunks:
            for n, base in enumerate(chunk):
                for s, value in enumerate((sources[pos + n][0], sources[pos + len(chunk)][n])):
                    spot = lax.bitwise_xor(at[0], jnp.int32(base ^ s)) ^ (at[1] & 1)
                    own = lax.dynamic_update_index_in_dim(own, value, spot, 0)
            pos += len(chunk) + 1
        sources.append(lax.all_gather(own, "gx", axis=0, tiled=True))
    theirs, mine = couple(at, table, lists, sources, (planes, nz, most, held, chunks, bases), nx * planes)
    local = {base: partner(x, base) for base, x in zip(bases, join(mine, family(theirs, 1)))}

    groups = child_coef.shape[1]
    chunks = tuple((base,) for base in bases[:half]) + (bases[half:],)
    order = range(len(chunks))
    nearest = len(chunks) - 1
    pieces = {(c, 0): stack([local[base] for base in chunks[c]]) for c in order}
    bits = [1 << n for n in range(fam.bit_length() - 2, -1, -1)]
    final = nearest - 1
    for c in [nearest] + list(order[:-1]):
        for bit in bits:
            for rel in sorted(r for g, r in pieces if g == c):
                if c != final or bit == fam // 2 or not rel & (fam // 2):
                    pieces[c, rel ^ bit] = family(pieces[c, rel], bit)
    last = [(final, rel) for rel in range(fam) if rel & (fam // 2)]
    soon = [key for key in pieces if key not in last]

    def work(keys):
        return tuple((rel, chunks[c]) for c, rel in keys)

    first = down(at, child_dir, mats, work(soon), [pieces[key] for key in soon], groups)
    pieces[last[0]], first = lax.optimization_barrier((pieces[last[0]], first))
    for bit in bits[1:]:
        for rel in sorted(r for g, r in pieces if g == final and r & (fam // 2)):
            pieces[final, rel ^ bit] = family(pieces[final, rel], bit)
    return down(at, child_dir, mats, work(last), [pieces[key] for key in last], groups, before=first)


def solution(mesh):
    return jax.shard_map(
        functools.partial(body, mesh.shape["gx"], mesh.shape["gy"]),
        mesh=mesh,
        in_specs=(
            P(("gx", "gy"), None, None, None),
            P(("gx", "gy"), None, None, None, None),
            P(("gx", "gy"), None),
            P("gx", "gy", None),
            P("gx", "gy", None),
            P("gx", "gy"),
            P("gy", None, None, None, None),
        ),
        out_specs=P(("gx", "gy"), None, None, None),
        check_vma=False,
    )
```

```python
import functools

import jax
import jax.numpy as jnp
from jax import lax
from jax.experimental import pallas as pl
from jax.experimental.pallas import tpu as pltpu
from jax.sharding import PartitionSpec as P

F32 = jnp.float32
BF16 = jnp.bfloat16
SMEM = pl.BlockSpec(memory_space=pltpu.SMEM)
VMEM = pl.BlockSpec(memory_space=pltpu.VMEM)
ANY = pl.BlockSpec(memory_space=pl.ANY)
COST = pl.CostEstimate(flops=10000000000, bytes_accessed=1000000, transcendentals=0)
PARAMS = pltpu.CompilerParams(vmem_limit_bytes=16 << 20)


def turned(v):
    half = v.shape[-1] // 2
    return jnp.concatenate([-v[..., half:], v[..., :half]], axis=-1)


def turned_rows(v):
    half = v.shape[0] // 2
    return jnp.concatenate([-v[half:], v[:half]], axis=0)


def dot(a, b):
    return jnp.dot(a, b, preferred_element_type=F32)


def xor(a, b):
    return lax.bitwise_xor(a, jnp.int32(b))


def place(at_ref, planes, rel, base, core):
    turn = lax.bitwise_and(xor(at_ref[1], rel), jnp.int32(1))
    q = lax.bitwise_xor(xor(at_ref[0], base % planes), turn)
    return q, xor(at_ref[1], rel ^ core), xor(at_ref[2], base // planes)


def up_kernel(groups, at_ref, dir_hbm, coef_hbm, mat_hbm, table_hbm, *rest):
    outs, (dir_ref, coef_ref, mat_ref, dir_sem, coef_sem, mat_sem) = rest[:-6], rest[-6:]
    children, planes, fam, nz, per = mat_hbm.shape[:5]

    coef_copy = pltpu.make_async_copy(coef_hbm, coef_ref, coef_sem)
    coef_copy.start()
    dir_copy = pltpu.make_async_copy(dir_hbm, dir_ref, dir_sem)
    dir_copy.start()
    slots, flying = {}, []

    def start(group):
        copies = []
        for _, _, rel, bases in group:
            for base, core in [(base, core) for base in bases for core in range(2)]:
                key = (rel, core, base % planes)
                if key not in slots:
                    slots[key] = slot = len(slots)
                    q, j, _ = place(at_ref, planes, rel, base, core)
                    copies.append(pltpu.make_async_copy(mat_hbm.at[:, q, j], mat_ref.at[slot], mat_sem.at[slot]))
                    copies[-1].start()
        flying.append(copies)

    start(groups[0])
    coef_copy.wait()
    for group in groups[1:2]:
        start(group)
    dir_copy.wait()
    for number, group in enumerate(groups):
        for copy in flying[number]:
            copy.wait()
        if number + 2 < len(groups):
            start(groups[number + 2])
        elif number + 2 == len(groups):
            table_copy = pltpu.make_async_copy(table_hbm.at[pl.ds(at_ref[2] * per, per)], outs[-1], coef_sem)
            table_copy.start()
        for out, offset, rel, bases in group:
            for n, core in [(n, core) for n in range(len(bases)) for core in range(2)]:
                q, j, z = place(at_ref, planes, rel, bases[n], core)
                slot = slots[rel, core, bases[n] % planes]
                for m in range(per):
                    left, right = [], []
                    for c in range(children):
                        v = coef_ref[c, dir_ref[c, ((q * fam + j) * nz + z) * per + m]]
                        left += [mat_ref[slot, c, z, m, 0], mat_ref[slot, c, z, m, 1]]
                        right += [v, turned(v)]
                    total = dot(jnp.concatenate(left, axis=1), jnp.concatenate(right, axis=0))
                    outs[out][offset + n, core, m] = total.astype(BF16)
    table_copy.wait()


def up(at, dirs, coef, mats, table, chunks, outs, groups):
    children, planes, fam, nz, per, _, rank, _ = mats.shape
    width = coef.shape[-1]
    where, shapes = {}, []
    for n, names in enumerate(outs):
        size = 0
        for c, rel in names:
            where[c, rel] = (n, size)
            size += len(chunks[c])
        shapes.append(jax.ShapeDtypeStruct((size, 2, per, rank, width), BF16))
    jobs = [[where[c, rel] + (rel, chunks[c]) for c, rel in group] for group in groups]
    slots = 2 * fam * len({base % planes for bases in chunks for base in bases})
    *found, table = pl.pallas_call(
        functools.partial(up_kernel, jobs),
        out_shape=shapes + [jax.ShapeDtypeStruct((per,) + table.shape[1:], BF16)],
        in_specs=[SMEM, ANY, ANY, ANY, ANY],
        out_specs=[VMEM] * (len(outs) + 1),
        scratch_shapes=[
            pltpu.SMEM(dirs.shape, jnp.int32),
            pltpu.VMEM(coef.shape, BF16),
            pltpu.VMEM((slots, children, nz, per, 2, rank, rank), BF16),
            pltpu.SemaphoreType.DMA,
            pltpu.SemaphoreType.DMA,
            pltpu.SemaphoreType.DMA((slots,)),
        ],
        compiler_params=PARAMS,
        cost_estimate=COST,
    )(at, *[pltpu.with_memory_space_constraint(x, pltpu.HBM) for x in (dirs, coef, mats, table)])
    return {name: (found[n], offset) for name, (n, offset) in where.items()}, found, table


def total_of(refs, offsets, count):
    total = None
    for ref, offset in zip(refs, offsets):
        term = ref[offset : offset + count].astype(F32)
        total = term if total is None else total + term
    return total.astype(BF16)


def add_kernel(offsets, *refs):
    refs[-1][...] = total_of(refs[:-1], offsets, refs[-1].shape[0])


def add(pieces, count):
    return pl.pallas_call(
        functools.partial(add_kernel, tuple(offset for _, offset in pieces)),
        out_shape=jax.ShapeDtypeStruct((count,) + pieces[0][0].shape[1:], BF16),
        in_specs=[VMEM] * len(pieces),
        out_specs=VMEM,
        compiler_params=PARAMS,
        cost_estimate=COST,
    )(*[array for array, _ in pieces])


def part_kernel(offsets, *refs):
    lists, outs = refs[:2], refs[2 + len(offsets) :]
    total = total_of(refs[2 : 2 + len(offsets)], offsets, len(outs))
    rows = total.shape[2] * total.shape[3]
    for n, out in enumerate(outs):
        for core in range(2):
            out[core, :rows] = total[n, core].reshape(rows, total.shape[4])
            out[core, rows:] = lists[core][...]


def part(pieces, count, lists):
    _, _, per, rank, width = pieces[0][0].shape
    return pl.pallas_call(
        functools.partial(part_kernel, tuple(offset for _, offset in pieces)),
        out_shape=[jax.ShapeDtypeStruct((2, per * rank + lists[0].shape[0], width), BF16)] * count,
        in_specs=[VMEM] * (2 + len(pieces)),
        out_specs=[VMEM] * count,
        compiler_params=PARAMS,
        cost_estimate=COST,
    )(*lists, *[array for array, _ in pieces])


def stack_kernel(core, *refs):
    for n, ref in enumerate(refs[:-1]):
        refs[-1][n] = ref[...] if core is None else ref[core]


def stack(arrays, core=None):
    shape = arrays[0].shape if core is None else arrays[0].shape[1:]
    return pl.pallas_call(
        functools.partial(stack_kernel, core),
        out_shape=jax.ShapeDtypeStruct((len(arrays),) + shape, arrays[0].dtype),
        in_specs=[VMEM] * len(arrays),
        out_specs=VMEM,
        compiler_params=PARAMS,
        cost_estimate=COST,
    )(*arrays)


def join_kernel(own_ref, other_ref, *outs):
    for n, out in enumerate(outs):
        out[0] = own_ref[n]
        out[1] = other_ref[n]


def join(own, other):
    return pl.pallas_call(
        join_kernel,
        out_shape=[jax.ShapeDtypeStruct((2,) + own.shape[1:], own.dtype)] * own.shape[0],
        in_specs=[VMEM] * 2,
        out_specs=[VMEM] * own.shape[0],
        compiler_params=PARAMS,
        cost_estimate=COST,
    )(own, other)


def couple_kernel(sizes, at_ref, table_ref, own_ref, *refs):
    planes, nz, most, held, chunks, bases = sizes
    sources, (theirs_ref, mine_ref, wide, numbers, lists, sem) = refs[:-6], refs[-6:]
    me = lax.bitwise_and(at_ref[1], jnp.int32(1))
    per, _, _, rank, _ = table_ref.shape
    count = wide.shape[0] - 1
    held_by, pos = {}, 0
    for chunk in chunks:
        for n, base in enumerate(chunk):
            held_by[base] = (sources[pos + n].at[0], sources[pos + len(chunk)].at[n])
        pos += len(chunk) + 1
    gathered = sources[pos:]
    for z in range(nz):
        if z == 0:
            tile = own_ref[...].astype(F32)
        else:
            mine, theirs = (ref[per * rank :].astype(F32) for ref in held_by[z * planes])
            tile = jnp.where(me == 0, mine, theirs)
        row_of = lax.broadcasted_iota(jnp.int32, tile.shape, 0)
        for q in range(planes):
            row = jnp.where(row_of == at_ref[2] * planes + q, tile, 0.0)
            numbers[pl.ds(z * planes + q, 1)] = jnp.sum(row, axis=0, keepdims=True).astype(jnp.int32)
    copy = pltpu.make_async_copy(numbers, lists, sem)
    copy.start()
    parts = []
    if gathered:
        parts = [(t, gathered[0].at[t]) for t in range(gathered[0].shape[0])]
    else:
        for base, pair in held_by.items():
            for s, source in enumerate(pair):
                q = lax.bitwise_xor(xor(at_ref[0], base % planes), xor(me, s))
                parts.append((xor(at_ref[2], base // planes) * planes + q, source))
    for t, source in parts:
        for m in range(per):
            v = source[m * rank : (m + 1) * rank]
            wide[t, m, :rank] = v
            wide[t, m, rank:] = turned(v)
    wide[count] = jnp.zeros_like(wide[count])
    copy.wait()
    for row, s in ((theirs_ref, 1), (mine_ref, 0)):
        for n, base in enumerate(bases):
            q = lax.bitwise_xor(xor(at_ref[0], base % planes), xor(me, s))
            for m in range(per):
                line, column = base // planes * planes + q, m * (2 * most + 1)
                active = lists[line, column + 2 * most]
                total = None
                for k in range(most):
                    kind = lists[line, column + most + k]
                    source = jnp.where(k < active, lists[line, column + k], count)
                    both = jnp.concatenate([table_ref[m, kind, 0], table_ref[m, kind, 1]], axis=1)
                    term = dot(both, wide[source, m])
                    total = term if total is None else total + term
                row[n, m] = total.T.astype(BF16)


def couple(at, table, own, sources, sizes, total):
    per, _, _, rank, _ = table.shape
    width = sources[0].shape[-1]
    listed = (sizes[0] * sizes[1], own.shape[1])
    rows = len(sizes[-1])
    return pl.pallas_call(
        functools.partial(couple_kernel, sizes),
        out_shape=[jax.ShapeDtypeStruct((rows, per, width, rank), BF16)] * 2,
        in_specs=[SMEM] + [VMEM] * (2 + len(sources)),
        out_specs=[VMEM] * 2,
        scratch_shapes=[
            pltpu.VMEM((total + 1, per, 2 * rank, width), BF16),
            pltpu.VMEM(listed, jnp.int32),
            pltpu.SMEM(listed, jnp.int32),
            pltpu.SemaphoreType.DMA,
        ],
        compiler_params=PARAMS,
        cost_estimate=COST,
    )(at, table, own, *sources)


def down_kernel(jobs, last, at_ref, dir_ref, mat_ref, *rest):
    pieces = rest[: len(jobs)]
    if last:
        before, out_ref, sums, staged, sems = rest[len(jobs) :]
    else:
        (sums,) = rest[len(jobs) :]
    children, planes, fam, nz, per, _, rank, _ = mat_ref.shape
    sums[...] = jnp.zeros_like(sums)
    for piece, (rel, bases) in zip(pieces, jobs):
        for n, core in [(n, core) for n in range(len(bases)) for core in range(2)]:
            q, j, z = place(at_ref, planes, rel, bases[n], core)
            for m in range(per):
                e = ((q * fam + j) * nz + z) * per + m
                v = piece[n, core, m]
                x = jnp.concatenate([v, turned_rows(v)], axis=1)
                both = [mat_ref[c, q, j, z, m].reshape(2 * rank, rank) for c in range(children)]
                y = dot(x, jnp.concatenate(both, axis=1))
                for c in range(children):
                    sums[c, dir_ref[c, e]] += y[:, c * rank : (c + 1) * rank]
    if last:
        copies = []
        for c in range(children):
            for i in range(staged.shape[1]):
                staged[c, i] = (sums[c, i] + before[c, i]).T.astype(BF16)
            copies.append(pltpu.make_async_copy(staged.at[c], out_ref.at[c], sems.at[c]))
            copies[-1].start()
        for copy in copies:
            copy.wait()


def down(at, dirs, mats, jobs, pieces, groups, before=None):
    children, rank = mats.shape[0], mats.shape[-1]
    width = pieces[0].shape[-2]
    last = before is not None
    sums = (children, groups, width, rank)
    return pl.pallas_call(
        functools.partial(down_kernel, jobs, last),
        out_shape=jax.ShapeDtypeStruct((children, groups, rank, width), BF16) if last else jax.ShapeDtypeStruct(sums, F32),
        in_specs=[SMEM, SMEM] + [VMEM] * (1 + len(pieces) + (1 if last else 0)),
        out_specs=ANY if last else VMEM,
        scratch_shapes=[
            pltpu.VMEM(sums, F32),
            pltpu.VMEM((children, groups, rank, width), BF16),
            pltpu.SemaphoreType.DMA((children,)),
        ]
        if last
        else [],
        compiler_params=PARAMS,
        cost_estimate=COST,
    )(at, dirs, mats, *pieces, *([before] if last else []))


def body(nx, ny, child_coef, transfer, child_dir, couple_src, couple_kind, couple_count, couple_table):
    children, dirs, _, rank, _ = transfer.shape
    planes, held, most = couple_src.shape
    fam = ny // planes
    split = held % nx == 0
    nz = nx if split else 1
    per = held // nz
    partners = nz * planes
    at_y, at_x = lax.axis_index("gy"), lax.axis_index("gx")
    at = jnp.stack([at_y // fam, at_y % fam, at_x if split else jnp.zeros_like(at_x)]).astype(jnp.int32)
    mats = transfer.reshape(children, planes, fam, nz, per, 2, rank, rank)
    bases = tuple(range(partners - 2, -1, -2))
    half = len(bases) // 2
    chunks = tuple((base,) for pair in zip(bases[:half], bases[half:]) for base in pair)

    def family(x, rel):
        return lax.ppermute(x, "gy", [(i, i ^ rel) for i in range(ny)])

    def partner(x, base):
        moves = [(r // planes) * ny + (r % planes) * fam for r in (base, base ^ 1)]
        axes, size = (("gx", "gy"), nx * ny) if split else ("gy", ny)
        return lax.ppermute(x, axes, [(i, i ^ moves[i & 1]) for i in range(size)])

    nearest = len(chunks) - 1
    order = range(len(chunks))
    top = fam - 1
    lead = [(c, top) for c in order[:-1]]
    rest = [(c, rel) for c in order for rel in range(1, fam, 2) if (c, rel) not in lead]
    keep = [(c, rel) for rel in range(fam - 2, -1, -2) for c in order]
    groups = [[(c, rel) for c in order] for rel in sorted(range(fam), key=lambda r: (-r, r))]
    sums, found, table = up(at, child_dir, child_coef, mats, couple_table, chunks, [lead, rest] + [[k] for k in keep], groups)
    got = {key: [sums[key]] for key in keep}
    for array, names in ((found[0], lead), (found[1], rest)):
        moved = family(array, 1)
        for c, rel in names:
            got[c, rel ^ 1].append((moved, sums[c, rel][1]))
    for bit in (1 << n for n in range(1, fam.bit_length() - 1)):
        for c in order:
            for rel in range(fam - 2, 0, -2):
                if rel & -rel == bit:
                    ready = add(got.pop((c, rel)), len(chunks[c]))
                    if bit == fam // 2:
                        ready, couple_src, couple_kind, couple_count = lax.optimization_barrier(
                            (ready, couple_src, couple_kind, couple_count)
                        )
                    moved = family(ready, bit)
                    got[c, rel ^ bit].append((moved, 0))
    lists = jnp.concatenate([couple_src, couple_kind, couple_count[..., None]], axis=-1)
    lists = lists.reshape(planes, nz, -1).transpose(1, 0, 2).reshape(partners, -1)
    lists = jnp.pad(lists, ((0, -partners % 16), (0, rank - lists.shape[1]))).astype(BF16)
    both_lists = (lists, family(lists, 1))
    sources = []
    for c in order:
        arrived = [partner(x, base) for x, base in zip(part(got[c, 0], len(chunks[c]), both_lists), chunks[c])]
        sources += arrived + [family(stack(arrived, core=1), 1)]
    if not split:
        own = jnp.zeros((partners,) + sources[0].shape[1:], BF16)
        pos = 0
        for chunk in chunks:
            for n, base in enumerate(chunk):
                for s, value in enumerate((sources[pos + n][0], sources[pos + len(chunk)][n])):
                    spot = lax.bitwise_xor(at[0], jnp.int32(base ^ s)) ^ (at[1] & 1)
                    own = lax.dynamic_update_index_in_dim(own, value, spot, 0)
            pos += len(chunk) + 1
        sources.append(lax.all_gather(own, "gx", axis=0, tiled=True))
    theirs, mine = couple(at, table, lists, sources, (planes, nz, most, held, chunks, bases), nx * planes)
    local = {base: partner(x, base) for base, x in zip(bases, join(mine, family(theirs, 1)))}

    groups = child_coef.shape[1]
    chunks = tuple((base,) for base in bases[:half]) + (bases[half:],)
    order = range(len(chunks))
    nearest = len(chunks) - 1
    pieces = {(c, 0): stack([local[base] for base in chunks[c]]) for c in order}
    bits = [1 << n for n in range(fam.bit_length() - 2, -1, -1)]
    final = nearest - 1
    for c in [nearest] + list(order[:-1]):
        for bit in bits:
            for rel in sorted(r for g, r in pieces if g == c):
                if c != final or bit == fam // 2 or not rel & (fam // 2):
                    pieces[c, rel ^ bit] = family(pieces[c, rel], bit)
    last = [(final, rel) for rel in range(fam) if rel & (fam // 2)]
    soon = [key for key in pieces if key not in last]

    def work(keys):
        return tuple((rel, chunks[c]) for c, rel in keys)

    first = down(at, child_dir, mats, work(soon), [pieces[key] for key in soon], groups)
    pieces[last[0]], first = lax.optimization_barrier((pieces[last[0]], first))
    for bit in bits[1:]:
        for rel in sorted(r for g, r in pieces if g == final and r & (fam // 2)):
            pieces[final, rel ^ bit] = family(pieces[final, rel], bit)
    return down(at, child_dir, mats, work(last), [pieces[key] for key in last], groups, before=first)


def solution(mesh):
    return jax.shard_map(
        functools.partial(body, mesh.shape["gx"], mesh.shape["gy"]),
        mesh=mesh,
        in_specs=(
            P(("gx", "gy"), None, None, None),
            P(("gx", "gy"), None, None, None, None),
            P(("gx", "gy"), None),
            P("gx", "gy", None),
            P("gx", "gy", None),
            P("gx", "gy"),
            P("gy", None, None, None, None),
        ),
        out_specs=P(("gx", "gy"), None, None, None),
        check_vma=False,
    )
```
